512 devices in a mesh: member: 16 (over y, x), band: 16 (over z), rep: 2 (over core).
Axes of the slice: x: 4, y: 4, z: 16, core: 2. Of those that a mesh axis runs over, the one named last changes fastest.
Arguments:
- features: bfloat16 [2, 16, 512, 128, 128], P('rep', 'member', None, 'band'), may hold values from -6 to 6
- kernel: bfloat16 [3, 3, 512, 90], replicated, may hold values from -0.09375 to 0.09375
- noise_seed: int32 [2, 16], P('rep', 'member'), may hold values from 0 to 31
- noise_table: float32 [32, 90], replicated, may hold values from -4 to 4
- truth: bfloat16 [2, 90, 128, 128], P('rep', None, 'band'), may hold values from -6 to 6
- area_weight: float32 [128], P('band'), may hold values from 0.1 to 1
Outputs:
- feature_grad: bfloat16 [2, 16, 512, 128, 128], P('rep', 'member', None, 'band')
- kernel_grad: float32 [3, 3, 512, 90], replicated
The draws below stay inside these ranges and needn't reach their ends.
All inputs are finite; a program needn't handle non-finite values.
Results may differ from the reference program's by a relative error of at most 0.014.
Values may be sent and summed in bfloat16 or wider, within the bound.
No kernel may reach another device: no remote copies, remote signals or barrier semaphores. Data moves between devices by JAX's collectives and lax.ppermute only.
A program may use at most 64 MiB of HBM per device.

```python
import math
import jax
import jax.numpy as jnp
from jax import lax

HID = 512
CHAN = 90
NOISE_ROWS = 32
LON = 128
ROWS = 128
MEMBERS = 16
DATES = 2


def touch_ends(values, key, least, high):
    shape = values.shape
    spot = [jax.random.randint(jax.random.fold_in(key, axis), (), 0, shape[axis]) for axis in range(len(shape))]
    values = values.at[tuple(spot)].set(least)
    longest = shape.index(max(shape))
    spot[longest] = (spot[longest] + 1) % shape[longest]
    return values.at[tuple(spot)].set(high)


def level_of(own_key, dims, split, smallest, high):
    loudness = 1.0
    for position, blocks in split:
        draws = jax.random.uniform(jax.random.fold_in(jax.random.fold_in(own_key, 6), position), (blocks,), jnp.float32, smallest / len(split), high / len(split))
        loudness = loudness * jnp.repeat(jnp.exp(draws), dims[position] // blocks).reshape((-1,) + (1,) * (len(dims) - 1 - position))
    return loudness


def gaussian(own_key, shape, scale, limit, split=(), held_as=jnp.bfloat16):
    values = scale * jax.random.normal(own_key, shape, jnp.float32)
    if split:
        values = values * level_of(own_key, shape, split, -0.22, 0.18)
    return jnp.clip(values, -limit, limit).astype(held_as)


def setup_inputs(seed: int = 0) -> dict:
    keys = jax.random.split(jax.random.key(seed), 7)
    features = gaussian(keys[0], (DATES, MEMBERS, HID, ROWS, LON), 1.0, 6.0, ((0, 2), (1, 16), (3, 16)))
    kernel = gaussian(keys[1], (3, 3, HID, CHAN), (9 * HID) ** -0.5, 0.09375)
    noise_seed = touch_ends(jax.random.randint(keys[2], (DATES, MEMBERS), 0, NOISE_ROWS), jax.random.fold_in(keys[2], 1), 0, NOISE_ROWS - 1).astype(jnp.int32)
    noise_table = gaussian(keys[3], (NOISE_ROWS, CHAN), 0.7, 4.0, (), jnp.float32)
    truth = gaussian(keys[4], (DATES, CHAN, ROWS, LON), 1.0, 6.0, ((0, 2), (2, 16)))
    area_weight = jnp.clip(jnp.exp(math.log(1.0) - 2.3025851 * jax.random.uniform(keys[5], (ROWS,), jnp.float32) ** level_of(keys[5], (ROWS,), ((0, 16),), -0.2, 0.2)), 0.1, 1.0)
    return dict(features=features, kernel=kernel, noise_seed=noise_seed, noise_table=noise_table, truth=truth, area_weight=area_weight)


smoothing = 0.1
alpha_level = 0.95

def slope(values):
    return values / jnp.sqrt(values * values + smoothing * smoothing)

def padded_map(field):
    return jnp.pad(field.astype(jnp.float32), ((0, 0), (1, 1), (1, 1)))

def forward_map(feature_map, kernel, offset):
    padded = padded_map(feature_map)
    result = jnp.zeros((CHAN, ROWS, LON), jnp.float32) + offset[:, None, None]
    for tap_row in range(3):
        for tap_col in range(3):
            result = result + jnp.einsum('hc,hrl->crl', kernel[tap_row, tap_col].astype(jnp.float32), padded[:, tap_row:tap_row + ROWS, tap_col:tap_col + LON], precision=lax.Precision.HIGHEST)
    return result

def reference(features, kernel, noise_seed, noise_table, truth, area_weight):
    flat_features = features.reshape(DATES * MEMBERS, HID, ROWS, LON)
    flat_seeds = noise_seed.reshape(DATES * MEMBERS)

    def predict(item):
        feature_map, seed_value = item
        return forward_map(feature_map, kernel, noise_table[seed_value])
    predicted = lax.map(predict, (flat_features, flat_seeds))
    by_date = predicted.reshape(DATES, MEMBERS, CHAN, ROWS, LON)
    date_ids = (jnp.arange(DATES * MEMBERS, dtype=jnp.int32) // MEMBERS).astype(jnp.int32)
    eps_value = (1.0 - alpha_level) / MEMBERS
    coef = (1.0 - eps_value) / (MEMBERS - 1)
    kernel_f = kernel.astype(jnp.float32)

    def backward(carry, item):
        own, date_id, feature_map = item
        others = by_date[date_id]
        pairs = lax.optimization_barrier(jnp.sum(slope(own[None] - others), axis=0))
        target = truth[date_id].astype(jnp.float32)
        delta = (area_weight[None, :, None] * (slope(own - target) - coef * pairs)).astype(jnp.bfloat16)
        delta_f = delta.astype(jnp.float32)
        delta_pad = padded_map(delta)
        padded = padded_map(feature_map)
        grad_map = jnp.zeros((HID, ROWS, LON), jnp.float32)
        tap_terms = []
        for tap_row in range(3):
            row_terms = []
            for tap_col in range(3):
                grad_map = grad_map + jnp.einsum('hc,crl->hrl', kernel_f[tap_row, tap_col], delta_pad[:, 2 - tap_row:2 - tap_row + ROWS, 2 - tap_col:2 - tap_col + LON], precision=lax.Precision.HIGHEST)
                row_terms.append(jnp.einsum('hrl,crl->hc', padded[:, tap_row:tap_row + ROWS, tap_col:tap_col + LON], delta_f, precision=lax.Precision.HIGHEST))
            tap_terms.append(jnp.stack(row_terms))
        return (carry + jnp.stack(tap_terms), grad_map.astype(jnp.bfloat16))
    start = jnp.zeros((3, 3, HID, CHAN), jnp.float32)
    total, grads = lax.scan(backward, start, (predicted, date_ids, flat_features))
    scale = 1.0 / math.sqrt(DATES * MEMBERS * ROWS * LON)
    kernel_grad = total * scale
    feature_grad = grads.reshape(DATES, MEMBERS, HID, ROWS, LON)
    return (feature_grad, kernel_grad)
```

```python
import functools
import math

import jax
import jax.numpy as jnp
from jax import lax
from jax.experimental import pallas as pl
from jax.experimental.pallas import tpu as pltpu
from jax.sharding import PartitionSpec as P

smoothing = 0.1
alpha_level = 0.95
padded_chans = 96
half_chans = padded_chans // 2
taps_chans = 3 * padded_chans
lanes = 128


def slope(values):
    return values * lax.rsqrt(values * values + smoothing * smoothing)


def shifted(block, step):
    lane = lax.broadcasted_iota(jnp.int32, block.shape, 1)
    width = block.shape[1]
    if step == 1:
        return jnp.where(lane == 0, 0.0, pltpu.roll(block, 1, 1))
    return jnp.where(lane == width - 1, 0.0, pltpu.roll(block, width - 1, 1))


def forward_kernel(x_ref, low_ref, high_ref, weight_ref, offset_ref, out_ref):
    rows = x_ref.shape[0]
    stack = [low_ref[...]] + [x_ref[row] for row in range(rows)] + [high_ref[...]]
    wide = jnp.concatenate(stack, axis=1)
    size = rows * lanes
    total = None
    for tap in range(3):
        part = jnp.dot(
            weight_ref[tap * taps_chans : (tap + 1) * taps_chans, :],
            wide[:, tap * lanes : tap * lanes + size],
            preferred_element_type=jnp.float32,
        )
        total = part if total is None else total + part
    offset = offset_ref[...]
    for row in range(rows):
        cell = total[:, row * lanes : (row + 1) * lanes]
        value = (
            cell[padded_chans : 2 * padded_chans]
            + shifted(cell[:padded_chans], 1)
            + shifted(cell[2 * padded_chans :], -1)
            + offset
        )
        out_ref[2 * row] = value[:half_chans]
        out_ref[2 * row + 1] = value[half_chans:]


def pair_kernel(coef, area_ref, values_ref, truth_ref, out_ref):
    members = values_ref.shape[0]
    weight = area_ref[0, 0]

    for step in range(half_chans // 16):
        deltas = [[] for _ in range(members)]
        for part in range(2):
            start = step * 16 + part * 8
            rows = slice(start, start + 8)
            values = [values_ref[member, rows, :] for member in range(members)]
            truth = truth_ref[rows, :]
            sums = [None] * members
            for one in range(members):
                for two in range(one + 1, members):
                    term = slope(values[one] - values[two])
                    sums[one] = term if sums[one] is None else sums[one] + term
                    sums[two] = -term if sums[two] is None else sums[two] - term
            for member in range(members):
                own = slope(values[member] - truth)
                deltas[member].append(weight * (own - coef * sums[member]))
        for member in range(members):
            both = jnp.concatenate(deltas[member], axis=0)
            out_ref[member, step * 16 : (step + 1) * 16, :] = both.astype(jnp.bfloat16)


def spread(block):
    exact = block.astype(jnp.float32)
    return [
        shifted(exact, -1).astype(jnp.bfloat16),
        block,
        shifted(exact, 1).astype(jnp.bfloat16),
    ]


def weight_grad_kernel(side_ref, x_ref, low_ref, high_ref, delta_ref, own_ref, other_ref, spread_ref, total_ref):
    rows = x_ref.shape[0]
    pieces = []
    for row in range(rows):
        block = jnp.concatenate([delta_ref[2 * row], delta_ref[2 * row + 1]], axis=0)
        pieces.append(jnp.concatenate(spread(block), axis=0))
    wide_delta = jnp.concatenate(pieces, axis=1)
    spread_ref[...] = wide_delta
    stack = [low_ref[...]] + [x_ref[row] for row in range(rows)] + [high_ref[...]]
    wide = jnp.concatenate(stack, axis=1)
    size = rows * lanes
    for tap in range(3):
        total_ref[tap * taps_chans : (tap + 1) * taps_chans, :] = lax.dot_general(
            wide_delta,
            wide[:, tap * lanes : tap * lanes + size],
            (((1,), (1,)), ((), ())),
            preferred_element_type=jnp.float32,
        )
    used = 3 * taps_chans
    total_ref[used:, :] = jnp.zeros((total_ref.shape[0] - used, total_ref.shape[1]), jnp.float32)
    side = side_ref[0, 0]
    half = total_ref.shape[1] // 2
    group = own_ref.shape[1]
    for target, start in ((own_ref, side * half), (other_ref, (1 - side) * half)):
        for part in range(2):
            column = pl.multiple_of(start + part * lanes, lanes)
            for block in range(own_ref.shape[0] // 2):
                target[2 * block + part] = total_ref[
                    block * group : (block + 1) * group, pl.ds(column, lanes)
                ].astype(jnp.bfloat16)


def feature_grad_kernel(weight_ref, spread_ref, low_ref, high_ref, out_ref):
    rows = out_ref.shape[0]
    size = rows * lanes
    ends = []
    for ref in (low_ref, high_ref):
        block = jnp.concatenate([ref[0], ref[1]], axis=0)
        ends.append(jnp.concatenate(spread(block), axis=0))
    wide = jnp.concatenate([ends[0], spread_ref[...], ends[1]], axis=1)
    deep = jnp.concatenate(
        [wide[:, (2 - tap) * lanes : (2 - tap) * lanes + size] for tap in range(3)], axis=0
    )
    result = lax.dot_general(
        weight_ref[...], deep, (((0,), (0,)), ((), ())), preferred_element_type=jnp.float32
    )
    for row in range(rows):
        out_ref[row] = result[:, row * lanes : (row + 1) * lanes].astype(jnp.bfloat16)


def finish_kernel(side_ref, own_ref, other_ref, out_ref):
    side = side_ref[0, 0]
    chans = out_ref.shape[1]
    half = out_ref.shape[2] // 2
    group = own_ref.shape[1]
    for source, start in ((own_ref, side * half), (other_ref, (1 - side) * half)):
        for part in range(2):
            column = pl.multiple_of(start + part * lanes, lanes)
            joined = jnp.concatenate(
                [source[2 * block + part] for block in range(source.shape[0] // 2)], axis=0
            ).astype(jnp.float32)
            for tap in range(out_ref.shape[0]):
                out_ref[tap, :, pl.ds(column, lanes)] = joined[
                    tap * padded_chans : tap * padded_chans + chans
                ]


vmem = pl.BlockSpec(memory_space=pltpu.VMEM)
smem = pl.BlockSpec(memory_space=pltpu.SMEM)


def call(kernel, out_shape, in_specs, scratch=(), limit=32):
    many = isinstance(out_shape, (list, tuple))
    return pl.pallas_call(
        kernel,
        out_shape=out_shape,
        in_specs=in_specs,
        out_specs=[vmem] * len(out_shape) if many else vmem,
        scratch_shapes=list(scratch),
        compiler_params=pltpu.CompilerParams(vmem_limit_bytes=limit * 1024 * 1024),
    )


def neighbours(low_edge, high_edge):
    count = lax.axis_size("band")
    forward = [(i, i + 1) for i in range(count - 1)]
    backward = [(target, source) for source, target in forward]
    return lax.ppermute(high_edge, "band", forward), lax.ppermute(low_edge, "band", backward)


def exchange(block, axis):
    return lax.all_to_all(block, axis, 0, 0, tiled=True)


def shared(block, axis):
    count = lax.axis_size(axis)
    return exchange(jnp.broadcast_to(block[None], (count,) + block.shape), axis)


def local(features, kernel, noise_seed, noise_table, truth, area_weight):
    feature_map = features[0, 0]
    hidden, rows, cols = feature_map.shape
    chans = kernel.shape[3]
    members = lax.axis_size("member")
    place = lax.axis_index("member")
    side = lax.axis_index("rep")
    bf16, f32 = jnp.bfloat16, jnp.float32

    x_low, x_high = neighbours(feature_map[:, 0, :], feature_map[:, rows - 1, :])
    x_rows = jnp.transpose(feature_map, (1, 0, 2))
    weights = jnp.pad(
        jnp.transpose(kernel, (0, 1, 3, 2)), ((0, 0), (0, 0), (0, padded_chans - chans), (0, 0))
    ).reshape(9 * padded_chans, hidden)
    offset = jnp.pad(
        lax.dynamic_slice(noise_table, (noise_seed[0, 0], 0), (1, chans))[0],
        (0, padded_chans - chans),
    )
    offset = jnp.broadcast_to(offset[:, None], (padded_chans, lanes))
    own_truth = jnp.pad(truth[0], ((0, padded_chans - chans), (0, 0), (0, 0)))
    own_truth = lax.dynamic_slice(
        own_truth, ((place % 2) * half_chans, place // 2, 0), (half_chans, 1, cols)
    )[:, 0, :].astype(f32)
    own_area = lax.dynamic_slice(area_weight, (place // 2,), (1,)).reshape(1, 1)
    side = jnp.full((1, 1), side, jnp.int32)

    predicted = call(
        forward_kernel,
        jax.ShapeDtypeStruct((members, half_chans, cols), f32),
        [vmem] * 5,
    )(x_rows, x_low, x_high, weights, offset)

    eps_value = (1.0 - alpha_level) / members
    coef = (1.0 - eps_value) / (members - 1)
    deltas = call(
        functools.partial(pair_kernel, coef),
        jax.ShapeDtypeStruct((members, half_chans, cols), bf16),
        [smem, vmem, vmem],
    )(own_area, exchange(predicted, "member"), own_truth)
    delta = exchange(deltas, "member")

    d_low, d_high = neighbours(delta[:2], delta[members - 2 :])
    group = 112
    piece = jax.ShapeDtypeStruct((16, group, lanes), bf16)
    own, other, wide_delta = call(
        weight_grad_kernel,
        [piece, piece, jax.ShapeDtypeStruct((taps_chans, rows * cols), bf16)],
        [smem] + [vmem] * 4,
        [pltpu.VMEM((8 * group, hidden), f32)],
    )(side, x_rows, x_low, x_high, delta)

    swap = [(0, 1), (1, 0)]
    other = lax.ppermute(other, "rep", swap)
    grad_rows = call(
        feature_grad_kernel,
        jax.ShapeDtypeStruct((rows, hidden, cols), bf16),
        [vmem] * 4,
    )(weights, wide_delta, d_low, d_high)
    feature_grad = jnp.transpose(grad_rows, (1, 0, 2))[None, None]

    part = (own.astype(f32) + other.astype(f32)).astype(bf16)
    part = jnp.sum(exchange(part, "member").astype(f32), axis=0).astype(bf16)
    scale = 1.0 / math.sqrt(lax.axis_size("rep") * members * lax.axis_size("band") * rows * cols)
    part = (jnp.sum(shared(part, "band").astype(f32), axis=0) * scale).astype(bf16)
    part = shared(part, "member")
    other = lax.ppermute(part, "rep", swap)
    kernel_grad = call(
        finish_kernel,
        jax.ShapeDtypeStruct((9, chans, hidden), f32),
        [smem, vmem, vmem],
    )(side, part, other)
    kernel_grad = jnp.transpose(kernel_grad.reshape(3, 3, chans, hidden), (0, 1, 3, 2))
    return (feature_grad, kernel_grad)


def solution(mesh):
    return jax.shard_map(
        local,
        mesh=mesh,
        in_specs=(
            P("rep", "member", None, "band", None),
            P(),
            P("rep", "member"),
            P(),
            P("rep", None, "band", None),
            P("band"),
        ),
        out_specs=(P("rep", "member", None, "band", None), P()),
        check_vma=False,
    )
```

```python
import functools
import math

import jax
import jax.numpy as jnp
from jax import lax
from jax.experimental import pallas as pl
from jax.experimental.pallas import tpu as pltpu
from jax.sharding import PartitionSpec as P

smoothing = 0.1
alpha_level = 0.95
padded_chans = 96
half_chans = padded_chans // 2
taps_chans = 3 * padded_chans
lanes = 128


def slope(values):
    return values * lax.rsqrt(values * values + smoothing * smoothing)


def shifted(block, step):
    lane = lax.broadcasted_iota(jnp.int32, block.shape, 1)
    width = block.shape[1]
    if step == 1:
        return jnp.where(lane == 0, 0.0, pltpu.roll(block, 1, 1))
    return jnp.where(lane == width - 1, 0.0, pltpu.roll(block, width - 1, 1))


def forward_kernel(x_ref, low_ref, high_ref, weight_ref, offset_ref, out_ref):
    rows = x_ref.shape[0]
    stack = [low_ref[...]] + [x_ref[row] for row in range(rows)] + [high_ref[...]]
    wide = jnp.concatenate(stack, axis=1)
    size = rows * lanes
    total = None
    for tap in range(3):
        part = jnp.dot(
            weight_ref[tap * taps_chans : (tap + 1) * taps_chans, :],
            wide[:, tap * lanes : tap * lanes + size],
            preferred_element_type=jnp.float32,
        )
        total = part if total is None else total + part
    offset = offset_ref[...]
    for row in range(rows):
        cell = total[:, row * lanes : (row + 1) * lanes]
        value = (
            cell[padded_chans : 2 * padded_chans]
            + shifted(cell[:padded_chans], 1)
            + shifted(cell[2 * padded_chans :], -1)
            + offset
        )
        out_ref[2 * row] = value[:half_chans]
        out_ref[2 * row + 1] = value[half_chans:]


def pair_kernel(coef, area_ref, values_ref, truth_ref, out_ref):
    members = values_ref.shape[0]
    weight = area_ref[0, 0]

    for step in range(half_chans // 16):
        deltas = [[] for _ in range(members)]
        for part in range(2):
            start = step * 16 + part * 8
            rows = slice(start, start + 8)
            values = [values_ref[member, rows, :] for member in range(members)]
            truth = truth_ref[rows, :]
            sums = [None] * members
            for one in range(members):
                for two in range(one + 1, members):
                    term = slope(values[one] - values[two])
                    sums[one] = term if sums[one] is None else sums[one] + term
                    sums[two] = -term if sums[two] is None else sums[two] - term
            for member in range(members):
                own = slope(values[member] - truth)
                deltas[member].append(weight * (own - coef * sums[member]))
        for member in range(members):
            both = jnp.concatenate(deltas[member], axis=0)
            out_ref[member, step * 16 : (step + 1) * 16, :] = both.astype(jnp.bfloat16)


def spread(block):
    exact = block.astype(jnp.float32)
    return [
        shifted(exact, -1).astype(jnp.bfloat16),
        block,
        shifted(exact, 1).astype(jnp.bfloat16),
    ]


def weight_grad_kernel(side_ref, x_ref, low_ref, high_ref, delta_ref, own_ref, other_ref, spread_ref, total_ref):
    rows = x_ref.shape[0]
    pieces = []
    for row in range(rows):
        block = jnp.concatenate([delta_ref[2 * row], delta_ref[2 * row + 1]], axis=0)
        pieces.append(jnp.concatenate(spread(block), axis=0))
    wide_delta = jnp.concatenate(pieces, axis=1)
    spread_ref[...] = wide_delta
    stack = [low_ref[...]] + [x_ref[row] for row in range(rows)] + [high_ref[...]]
    wide = jnp.concatenate(stack, axis=1)
    size = rows * lanes
    for tap in range(3):
        total_ref[tap * taps_chans : (tap + 1) * taps_chans, :] = lax.dot_general(
            wide_delta,
            wide[:, tap * lanes : tap * lanes + size],
            (((1,), (1,)), ((), ())),
            preferred_element_type=jnp.float32,
        )
    used = 3 * taps_chans
    total_ref[used:, :] = jnp.zeros((total_ref.shape[0] - used, total_ref.shape[1]), jnp.float32)
    side = side_ref[0, 0]
    half = total_ref.shape[1] // 2
    group = own_ref.shape[1]
    for target, start in ((own_ref, side * half), (other_ref, (1 - side) * half)):
        for part in range(2):
            column = pl.multiple_of(start + part * lanes, lanes)
            for block in range(own_ref.shape[0] // 2):
                target[2 * block + part] = total_ref[
                    block * group : (block + 1) * group, pl.ds(column, lanes)
                ].astype(jnp.bfloat16)


def feature_grad_kernel(weight_ref, spread_ref, low_ref, high_ref, out_ref):
    rows = out_ref.shape[0]
    size = rows * lanes
    ends = []
    for ref in (low_ref, high_ref):
        block = jnp.concatenate([ref[0], ref[1]], axis=0)
        ends.append(jnp.concatenate(spread(block), axis=0))
    wide = jnp.concatenate([ends[0], spread_ref[...], ends[1]], axis=1)
    deep = jnp.concatenate(
        [wide[:, (2 - tap) * lanes : (2 - tap) * lanes + size] for tap in range(3)], axis=0
    )
    result = lax.dot_general(
        weight_ref[...], deep, (((0,), (0,)), ((), ())), preferred_element_type=jnp.float32
    )
    for row in range(rows):
        out_ref[row] = result[:, row * lanes : (row + 1) * lanes].astype(jnp.bfloat16)


def join_kernel(own_ref, other_ref, out_ref):
    for block in range(own_ref.shape[0]):
        both = own_ref[block].astype(jnp.float32) + other_ref[block].astype(jnp.float32)
        out_ref[block] = both.astype(jnp.bfloat16)


def sum_kernel(scale, parts_ref, *refs):
    out_ref = refs[-1]
    total = parts_ref[0].astype(jnp.float32)
    for part in range(1, parts_ref.shape[0]):
        total = total + parts_ref[part].astype(jnp.float32)
    value = (total * scale).astype(jnp.bfloat16)
    for copy in range(out_ref.shape[0]):
        out_ref[copy] = value


def finish_kernel(side_ref, own_ref, other_ref, after_ref, out_ref):
    side = side_ref[0, 0]
    chans = out_ref.shape[1]
    half = out_ref.shape[2] // 2
    group = own_ref.shape[1]
    for source, start in ((own_ref, side * half), (other_ref, (1 - side) * half)):
        for part in range(2):
            column = pl.multiple_of(start + part * lanes, lanes)
            joined = jnp.concatenate(
                [source[2 * block + part] for block in range(source.shape[0] // 2)], axis=0
            ).astype(jnp.float32)
            for tap in range(out_ref.shape[0]):
                out_ref[tap, :, pl.ds(column, lanes)] = joined[
                    tap * padded_chans : tap * padded_chans + chans
                ]


vmem = pl.BlockSpec(memory_space=pltpu.VMEM)
smem = pl.BlockSpec(memory_space=pltpu.SMEM)
anywhere = pl.BlockSpec(memory_space=pl.ANY)


def call(kernel, out_shape, in_specs, scratch=(), limit=32, cost=(0, 0)):
    many = isinstance(out_shape, (list, tuple))
    return pl.pallas_call(
        kernel,
        out_shape=out_shape,
        in_specs=in_specs,
        out_specs=[vmem] * len(out_shape) if many else vmem,
        scratch_shapes=list(scratch),
        cost_estimate=pl.CostEstimate(flops=cost[0], bytes_accessed=cost[1], transcendentals=0),
        compiler_params=pltpu.CompilerParams(vmem_limit_bytes=limit * 1024 * 1024),
    )


def neighbours(low_edge, high_edge):
    count = lax.axis_size("band")
    forward = [(i, i + 1) for i in range(count - 1)]
    backward = [(target, source) for source, target in forward]
    return lax.ppermute(high_edge, "band", forward), lax.ppermute(low_edge, "band", backward)


def exchange(block, axis, groups=None):
    return lax.all_to_all(block, axis, 0, 0, axis_index_groups=groups, tiled=True)


def summed(parts, copies, scale=1.0, after=()):
    return call(
        functools.partial(sum_kernel, scale),
        jax.ShapeDtypeStruct((copies,) + parts.shape[1:], jnp.bfloat16),
        [vmem] + [anywhere] * len(after),
        cost=(parts.size, 2 * parts.size),
    )(parts, *after)


def local(features, kernel, noise_seed, noise_table, truth, area_weight):
    feature_map = features[0, 0]
    hidden, rows, cols = feature_map.shape
    chans = kernel.shape[3]
    members = lax.axis_size("member")
    place = lax.axis_index("member")
    side = lax.axis_index("rep")
    bf16, f32 = jnp.bfloat16, jnp.float32

    x_low, x_high = neighbours(feature_map[:, 0, :], feature_map[:, rows - 1, :])
    x_rows = jnp.transpose(feature_map, (1, 0, 2))
    weights = jnp.pad(
        jnp.transpose(kernel, (0, 1, 3, 2)), ((0, 0), (0, 0), (0, padded_chans - chans), (0, 0))
    ).reshape(9 * padded_chans, hidden)
    offset = jnp.pad(
        lax.dynamic_slice(noise_table, (noise_seed[0, 0], 0), (1, chans))[0],
        (0, padded_chans - chans),
    )
    offset = jnp.broadcast_to(offset[:, None], (padded_chans, lanes))
    own_truth = jnp.pad(truth[0], ((0, padded_chans - chans), (0, 0), (0, 0)))
    own_truth = lax.dynamic_slice(
        own_truth, ((place % 2) * half_chans, place // 2, 0), (half_chans, 1, cols)
    )[:, 0, :].astype(f32)
    own_area = lax.dynamic_slice(area_weight, (place // 2,), (1,)).reshape(1, 1)
    side = jnp.full((1, 1), side, jnp.int32)

    predicted = call(
        forward_kernel,
        jax.ShapeDtypeStruct((members, half_chans, cols), f32),
        [vmem] * 5,
        cost=(2 * hidden * 9 * chans * rows * cols, 4 * hidden * rows * cols),
    )(x_rows, x_low, x_high, weights, offset)

    eps_value = (1.0 - alpha_level) / members
    coef = (1.0 - eps_value) / (members - 1)
    deltas = call(
        functools.partial(pair_kernel, coef),
        jax.ShapeDtypeStruct((members, half_chans, cols), bf16),
        [smem, vmem, vmem],
        cost=(members * members * 8 * half_chans * cols, 6 * members * half_chans * cols),
    )(own_area, exchange(predicted, "member"), own_truth)
    delta = exchange(deltas, "member")

    d_low, d_high = neighbours(delta[:2], delta[members - 2 :])
    group = 112
    piece = jax.ShapeDtypeStruct((16, group, lanes), bf16)
    own, other, wide_delta = call(
        weight_grad_kernel,
        [piece, piece, jax.ShapeDtypeStruct((taps_chans, rows * cols), bf16)],
        [smem] + [vmem] * 4,
        [pltpu.VMEM((8 * group, hidden), f32)],
        cost=(2 * hidden * 9 * chans * rows * cols, 4 * hidden * rows * cols),
    )(side, x_rows, x_low, x_high, delta)

    swap = [(0, 1), (1, 0)]
    other = lax.ppermute(other, "rep", swap)
    grad_rows = call(
        feature_grad_kernel,
        jax.ShapeDtypeStruct((rows, hidden, cols), bf16),
        [vmem] * 4,
        cost=(2 * hidden * 9 * chans * rows * cols, 4 * hidden * rows * cols),
    )(weights, wide_delta, d_low, d_high)
    feature_grad = jnp.transpose(grad_rows, (1, 0, 2))[None, None]

    part = call(
        join_kernel,
        jax.ShapeDtypeStruct((members, group, lanes), bf16),
        [vmem, vmem],
        cost=(own.size, 6 * own.size),
    )(own, other)
    bands = lax.axis_size("band")
    near = 4
    far = bands // near
    nearby = [[far_step * near + step for step in range(near)] for far_step in range(far)]
    distant = [[far_step * near + step for far_step in range(far)] for step in range(near)]
    part = summed(exchange(part, "member"), far)
    part = summed(exchange(part, "band", distant), near, after=(d_low, d_high))
    scale = 1.0 / math.sqrt(lax.axis_size("rep") * members * bands * rows * cols)
    part = summed(exchange(part, "band", nearby), members, scale)
    part = exchange(part, "member")
    other = lax.ppermute(part, "rep", swap)
    kernel_grad = call(
        finish_kernel,
        jax.ShapeDtypeStruct((9, chans, hidden), f32),
        [smem, vmem, vmem, anywhere],
    )(side, part, other, feature_grad)
    kernel_grad = jnp.transpose(kernel_grad.reshape(3, 3, chans, hidden), (0, 1, 3, 2))
    return (feature_grad, kernel_grad)


def solution(mesh):
    return jax.shard_map(
        local,
        mesh=mesh,
        in_specs=(
            P("rep", "member", None, "band", None),
            P(),
            P("rep", "member"),
            P(),
            P("rep", None, "band", None),
            P("band"),
        ),
        out_specs=(P("rep", "member", None, "band", None), P()),
        check_vma=False,
    )
```

```python
import functools
import math

import jax
import jax.numpy as jnp
from jax import lax
from jax.experimental import pallas as pl
from jax.experimental.pallas import tpu as pltpu
from jax.sharding import PartitionSpec as P

smoothing = 0.1
alpha_level = 0.95
padded_chans = 96
half_chans = padded_chans // 2
taps_chans = 3 * padded_chans
lanes = 128
padded_rows = 896


def slope(values):
    return values * lax.rsqrt(values * values + smoothing * smoothing)


def shifted(block, step):
    lane = lax.broadcasted_iota(jnp.int32, block.shape, 1)
    width = block.shape[1]
    if step == 1:
        return jnp.where(lane == 0, 0.0, pltpu.roll(block, 1, 1))
    return jnp.where(lane == width - 1, 0.0, pltpu.roll(block, width - 1, 1))


def folded(sums):
    return (
        sums[padded_chans : 2 * padded_chans]
        + shifted(sums[:padded_chans], 1)
        + shifted(sums[2 * padded_chans :], -1)
    )


def inner_kernel(x_ref, weight_ref, offset_ref, truth_ref, out_ref):
    rows = x_ref.shape[0]
    wide = jnp.concatenate([x_ref[row] for row in range(rows)], axis=1)
    sums = [
        jnp.dot(
            weight_ref[tap * taps_chans : (tap + 1) * taps_chans, :],
            wide[:, max(tap - 1, 0) * lanes : (rows + min(tap - 1, 0)) * lanes],
            preferred_element_type=jnp.float32,
        )
        for tap in range(3)
    ]
    offset = offset_ref[...]
    for row in range(rows):
        cell = sums[1][:, row * lanes : (row + 1) * lanes]
        if row > 0:
            cell = cell + sums[0][:, (row - 1) * lanes : row * lanes]
        if row < rows - 1:
            cell = cell + sums[2][:, row * lanes : (row + 1) * lanes]
        value = folded(cell) + offset
        out_ref[2 * row] = value[:half_chans]
        out_ref[2 * row + 1] = value[half_chans:]


def edge_kernel(inner_ref, low_ref, high_ref, weight_ref, out_ref):
    chunks = inner_ref.shape[0]
    for chunk in range(2, chunks - 2):
        out_ref[chunk] = inner_ref[chunk]
    for tap, ref, first in ((0, low_ref, 0), (2, high_ref, chunks - 2)):
        value = folded(
            jnp.dot(
                weight_ref[tap * taps_chans : (tap + 1) * taps_chans, :],
                ref[...],
                preferred_element_type=jnp.float32,
            )
        )
        out_ref[first] = inner_ref[first] + value[:half_chans]
        out_ref[first + 1] = inner_ref[first + 1] + value[half_chans:]


def pair_kernel(coef, values_ref, truth_ref, area_ref, out_ref, delta_ref):
    members = values_ref.shape[0]
    lane = lax.broadcasted_iota(jnp.int32, area_ref.shape, 1)
    row = lax.axis_index("member") // 2
    weight = jnp.sum(jnp.where(lane == row, area_ref[...], 0.0), axis=1, keepdims=True)
    weight = jnp.broadcast_to(weight, (8, lanes))
    for start in range(0, half_chans, 8):
        rows = slice(start, start + 8)
        values = [values_ref[member, rows, :] for member in range(members)]
        truth = truth_ref[rows, :]
        sums = [None] * members
        for one in range(members):
            for two in range(one + 1, members):
                term = slope(values[one] - values[two])
                sums[one] = term if sums[one] is None else sums[one] + term
                sums[two] = -term if sums[two] is None else sums[two] - term
        for member in range(members):
            own = slope(values[member] - truth)
            delta_ref[member, rows, :] = weight * (own - coef * sums[member])
    for member in range(members):
        out_ref[member] = delta_ref[member].astype(jnp.bfloat16)


def spread(block):
    exact = block.astype(jnp.float32)
    return [
        shifted(exact, -1).astype(jnp.bfloat16),
        block,
        shifted(exact, 1).astype(jnp.bfloat16),
    ]


def taps_product(wide_delta, side, x_ref, low_ref, high_ref):
    rows, hidden = x_ref.shape[:2]
    half = hidden // 2
    mine = pl.ds(pl.multiple_of(side * half, half), half)
    stack = [low_ref[mine, :]] + [x_ref[row, mine, :] for row in range(rows)] + [high_ref[mine, :]]
    wide = jnp.concatenate(stack, axis=1)
    size = rows * lanes
    parts = [
        lax.dot_general(
            wide_delta,
            wide[:, tap * lanes : tap * lanes + size],
            (((1,), (1,)), ((), ())),
            preferred_element_type=jnp.float32,
        )
        for tap in range(3)
    ]
    parts.append(jnp.zeros((padded_rows - 3 * taps_chans, half), jnp.float32))
    return jnp.concatenate(parts, axis=0)


def sent_kernel(delta_ref, x_ref, low_ref, high_ref, out_ref, spread_ref):
    pieces = []
    for row in range(x_ref.shape[0]):
        block = jnp.concatenate([delta_ref[2 * row], delta_ref[2 * row + 1]], axis=0)
        pieces.append(jnp.concatenate(spread(block), axis=0))
    wide_delta = jnp.concatenate(pieces, axis=1)
    spread_ref[...] = wide_delta
    side = 1 - lax.axis_index("rep")
    total = taps_product(wide_delta, side, x_ref, low_ref, high_ref)
    group = out_ref.shape[1]
    for block in range(out_ref.shape[0]):
        out_ref[block] = total[
            block // 2 * group : (block // 2 + 1) * group,
            block % 2 * lanes : (block % 2 + 1) * lanes,
        ].astype(jnp.bfloat16)


def kept_kernel(spread_ref, x_ref, low_ref, high_ref, other_ref, out_ref):
    side = lax.axis_index("rep")
    total = taps_product(spread_ref[...], side, x_ref, low_ref, high_ref)
    group = out_ref.shape[1]
    for block in range(out_ref.shape[0]):
        own = total[
            block // 2 * group : (block // 2 + 1) * group,
            block % 2 * lanes : (block % 2 + 1) * lanes,
        ]
        out_ref[block] = (own + other_ref[block].astype(jnp.float32)).astype(jnp.bfloat16)


def feature_grad_kernel(weight_ref, spread_ref, low_ref, high_ref, out_ref):
    rows = out_ref.shape[0]
    size = rows * lanes
    ends = []
    for ref in (low_ref, high_ref):
        block = jnp.concatenate([ref[0], ref[1]], axis=0)
        ends.append(jnp.concatenate(spread(block), axis=0))
    wide = jnp.concatenate([ends[0], spread_ref[...], ends[1]], axis=1)
    deep = jnp.concatenate(
        [wide[:, (2 - tap) * lanes : (2 - tap) * lanes + size] for tap in range(3)], axis=0
    )
    result = lax.dot_general(
        weight_ref[...], deep, (((0,), (0,)), ((), ())), preferred_element_type=jnp.float32
    )
    for row in range(rows):
        out_ref[row] = result[:, row * lanes : (row + 1) * lanes].astype(jnp.bfloat16)


def sum_kernel(scale, parts_ref, *refs):
    out_ref = refs[-1]
    total = parts_ref[0].astype(jnp.float32)
    for part in range(1, parts_ref.shape[0]):
        total = total + parts_ref[part].astype(jnp.float32)
    value = (total * scale).astype(jnp.bfloat16)
    for copy in range(out_ref.shape[0]):
        out_ref[copy] = value


def finish_kernel(away, source_ref, *refs):
    out_ref, block_ref, sem = refs[-3:]
    chans, half = block_ref.shape[1:]
    for part in range(2):
        joined = jnp.concatenate(
            [source_ref[2 * block + part] for block in range(source_ref.shape[0] // 2)], axis=0
        ).astype(jnp.float32)
        for tap in range(block_ref.shape[0]):
            block_ref[tap, :, part * lanes : (part + 1) * lanes] = joined[
                tap * padded_chans : tap * padded_chans + chans
            ]
    side = lax.axis_index("rep")
    side = 1 - side if away else side
    mine = pl.ds(pl.multiple_of(side * half, half), half)
    copy = pltpu.make_async_copy(block_ref, out_ref.at[:, :, mine], sem)
    copy.start()
    copy.wait()


vmem = pl.BlockSpec(memory_space=pltpu.VMEM)
anywhere = pl.BlockSpec(memory_space=pl.ANY)


def call(kernel, out_shape, in_specs, scratch=(), limit=32, cost=(0, 0)):
    many = isinstance(out_shape, (list, tuple))
    return pl.pallas_call(
        kernel,
        out_shape=out_shape,
        in_specs=in_specs,
        out_specs=[vmem] * len(out_shape) if many else vmem,
        scratch_shapes=list(scratch),
        cost_estimate=pl.CostEstimate(flops=cost[0], bytes_accessed=cost[1], transcendentals=0),
        compiler_params=pltpu.CompilerParams(vmem_limit_bytes=limit * 1024 * 1024),
    )


def neighbours(low_edge, high_edge):
    count = lax.axis_size("band")
    forward = [(i, i + 1) for i in range(count - 1)]
    backward = [(target, source) for source, target in forward]
    return lax.ppermute(high_edge, "band", forward), lax.ppermute(low_edge, "band", backward)


def exchange(block, axis, groups=None):
    return lax.all_to_all(block, axis, 0, 0, axis_index_groups=groups, tiled=True)


def summed(parts, copies, scale=1.0, after=()):
    return call(
        functools.partial(sum_kernel, scale),
        jax.ShapeDtypeStruct((copies,) + parts.shape[1:], jnp.bfloat16),
        [vmem] + [anywhere] * len(after),
        cost=(parts.size, 2 * parts.size),
    )(parts, *after)


def placed(away, source, shape, *before):
    return pl.pallas_call(
        functools.partial(finish_kernel, away),
        out_shape=jax.ShapeDtypeStruct(shape, jnp.float32),
        in_specs=[vmem] + [anywhere] * len(before),
        out_specs=anywhere,
        scratch_shapes=[
            pltpu.VMEM(shape[:2] + (shape[2] // 2,), jnp.float32),
            pltpu.SemaphoreType.DMA,
        ],
        input_output_aliases={1: 0} if before else {},
        cost_estimate=pl.CostEstimate(
            flops=source.size, bytes_accessed=6 * source.size, transcendentals=0
        ),
        compiler_params=pltpu.CompilerParams(vmem_limit_bytes=32 * 1024 * 1024),
    )(source, *before)


def local(features, kernel, noise_seed, noise_table, truth, area_weight):
    feature_map = features[0, 0]
    hidden, rows, cols = feature_map.shape
    chans = kernel.shape[3]
    members = lax.axis_size("member")
    place = lax.axis_index("member")
    bf16, f32 = jnp.bfloat16, jnp.float32

    x_low, x_high = neighbours(feature_map[:, 0, :], feature_map[:, rows - 1, :])
    x_rows = jnp.transpose(feature_map, (1, 0, 2))
    weights = jnp.pad(
        jnp.transpose(kernel, (0, 1, 3, 2)), ((0, 0), (0, 0), (0, padded_chans - chans), (0, 0))
    ).reshape(9 * padded_chans, hidden)
    offset = jnp.pad(
        lax.dynamic_slice(noise_table, (noise_seed[0, 0], 0), (1, chans))[0],
        (0, padded_chans - chans),
    )
    offset = jnp.broadcast_to(offset[:, None], (padded_chans, lanes))
    own_truth = jnp.pad(truth[0], ((0, padded_chans - chans), (0, 0), (0, 0)))
    own_truth = lax.dynamic_slice(
        own_truth, ((place % 2) * half_chans, place // 2, 0), (half_chans, 1, cols)
    )[:, 0, :].astype(f32)
    inner = call(
        inner_kernel,
        jax.ShapeDtypeStruct((members, half_chans, cols), f32),
        [vmem] * 3 + [anywhere],
        cost=(2 * hidden * 9 * chans * rows * cols, 4 * hidden * rows * cols),
    )(x_rows, weights, offset, own_truth)
    predicted = call(
        edge_kernel,
        jax.ShapeDtypeStruct((members, half_chans, cols), f32),
        [vmem] * 4,
        cost=(4 * hidden * 3 * chans * cols, 4 * hidden * cols),
    )(inner, x_low, x_high, weights)

    eps_value = (1.0 - alpha_level) / members
    coef = (1.0 - eps_value) / (members - 1)
    deltas = call(
        functools.partial(pair_kernel, coef),
        jax.ShapeDtypeStruct((members, half_chans, cols), bf16),
        [vmem] * 3,
        [pltpu.VMEM((members, half_chans, cols), f32)],
        cost=(members * members * 8 * half_chans * cols, 6 * members * half_chans * cols),
    )(exchange(predicted, "member"), own_truth, area_weight[None])
    delta = exchange(deltas, "member")

    d_low, d_high = neighbours(delta[:2], delta[members - 2 :])
    group = padded_rows // 8
    piece = jax.ShapeDtypeStruct((members, group, lanes), bf16)
    flops = hidden * 9 * chans * rows * cols
    sent, wide_delta = call(
        sent_kernel,
        [piece, jax.ShapeDtypeStruct((taps_chans, rows * cols), bf16)],
        [vmem] * 4,
        cost=(flops, 2 * hidden * rows * cols),
    )(delta, x_rows, x_low, x_high)
    swap = [(0, 1), (1, 0)]
    part = call(
        kept_kernel,
        piece,
        [vmem] * 5,
        cost=(flops, 2 * hidden * rows * cols),
    )(wide_delta, x_rows, x_low, x_high, lax.ppermute(sent, "rep", swap))
    grad_rows = call(
        feature_grad_kernel,
        jax.ShapeDtypeStruct((rows, hidden, cols), bf16),
        [vmem] * 4,
        cost=(2 * hidden * 9 * chans * rows * cols, 4 * hidden * rows * cols),
    )(weights, wide_delta, d_low, d_high)
    feature_grad = jnp.transpose(grad_rows, (1, 0, 2))[None, None]

    bands = lax.axis_size("band")
    near = 4
    far = bands // near
    nearby = [[far_step * near + step for step in range(near)] for far_step in range(far)]
    distant = [[far_step * near + step for far_step in range(far)] for step in range(near)]
    part = summed(exchange(part, "member"), far)
    part = summed(exchange(part, "band", distant), near, after=(d_low, d_high))
    scale = 1.0 / math.sqrt(lax.axis_size("rep") * members * bands * rows * cols)
    part = summed(exchange(part, "band", nearby), members, scale, after=(feature_grad,))
    part = exchange(part, "member")
    other = lax.ppermute(part, "rep", swap)
    kernel_grad = placed(False, part, (9, chans, hidden))
    kernel_grad = placed(True, other, (9, chans, hidden), kernel_grad)
    kernel_grad = jnp.transpose(kernel_grad.reshape(3, 3, chans, hidden), (0, 1, 3, 2))
    return (feature_grad, kernel_grad)


def solution(mesh):
    return jax.shard_map(
        local,
        mesh=mesh,
        in_specs=(
            P("rep", "member", None, "band", None),
            P(),
            P("rep", "member"),
            P(),
            P("rep", None, "band", None),
            P("band"),
        ),
        out_specs=(P("rep", "member", None, "band", None), P()),
        check_vma=False,
    )
```

```python
import functools
import math

import jax
import jax.numpy as jnp
from jax import lax
from jax.experimental import pallas as pl
from jax.experimental.pallas import tpu as pltpu
from jax.sharding import PartitionSpec as P

smoothing = 0.1
alpha_level = 0.95
padded_chans = 96
half_chans = padded_chans // 2
taps_chans = 3 * padded_chans
lanes = 128
padded_rows = 896


def slope(values):
    return values * lax.rsqrt(values * values + smoothing * smoothing)


def shifted(block, step):
    lane = lax.broadcasted_iota(jnp.int32, block.shape, 1)
    width = block.shape[1]
    if step == 1:
        return jnp.where(lane == 0, 0.0, pltpu.roll(block, 1, 1))
    return jnp.where(lane == width - 1, 0.0, pltpu.roll(block, width - 1, 1))


def folded(sums):
    return (
        sums[padded_chans : 2 * padded_chans]
        + shifted(sums[:padded_chans], 1)
        + shifted(sums[2 * padded_chans :], -1)
    )


def inner_kernel(x_ref, weight_ref, offset_ref, truth_ref, out_ref):
    rows = x_ref.shape[0]
    wide = jnp.concatenate([x_ref[row] for row in range(rows)], axis=1)
    sums = [
        jnp.dot(
            weight_ref[tap * taps_chans : (tap + 1) * taps_chans, :],
            wide[:, max(tap - 1, 0) * lanes : (rows + min(tap - 1, 0)) * lanes],
            preferred_element_type=jnp.float32,
        )
        for tap in range(3)
    ]
    offset = offset_ref[...]
    for row in range(rows):
        cell = sums[1][:, row * lanes : (row + 1) * lanes]
        if row > 0:
            cell = cell + sums[0][:, (row - 1) * lanes : row * lanes]
        if row < rows - 1:
            cell = cell + sums[2][:, row * lanes : (row + 1) * lanes]
        value = folded(cell) + offset
        out_ref[2 * row] = value[:half_chans]
        out_ref[2 * row + 1] = value[half_chans:]


def edge_kernel(inner_ref, low_ref, high_ref, weight_ref, out_ref):
    chunks = inner_ref.shape[0]
    for chunk in range(2, chunks - 2):
        out_ref[chunk] = inner_ref[chunk]
    for tap, ref, first in ((0, low_ref, 0), (2, high_ref, chunks - 2)):
        value = folded(
            jnp.dot(
                weight_ref[tap * taps_chans : (tap + 1) * taps_chans, :],
                ref[...],
                preferred_element_type=jnp.float32,
            )
        )
        out_ref[first] = inner_ref[first] + value[:half_chans]
        out_ref[first + 1] = inner_ref[first + 1] + value[half_chans:]


def pair_kernel(coef, values_ref, truth_ref, area_ref, out_ref, delta_ref):
    members = values_ref.shape[0]
    lane = lax.broadcasted_iota(jnp.int32, area_ref.shape, 1)
    row = lax.axis_index("member") // 2
    weight = jnp.sum(jnp.where(lane == row, area_ref[...], 0.0), axis=1, keepdims=True)
    weight = jnp.broadcast_to(weight, (8, lanes))
    for start in range(0, half_chans, 8):
        rows = slice(start, start + 8)
        values = [values_ref[member, rows, :] for member in range(members)]
        truth = truth_ref[rows, :]
        sums = [None] * members
        for one in range(members):
            for two in range(one + 1, members):
                term = slope(values[one] - values[two])
                sums[one] = term if sums[one] is None else sums[one] + term
                sums[two] = -term if sums[two] is None else sums[two] - term
        for member in range(members):
            own = slope(values[member] - truth)
            delta_ref[member, rows, :] = weight * (own - coef * sums[member])
    for member in range(members):
        out_ref[member] = delta_ref[member].astype(jnp.bfloat16)


def spread(block):
    exact = block.astype(jnp.float32)
    return [
        shifted(exact, -1).astype(jnp.bfloat16),
        block,
        shifted(exact, 1).astype(jnp.bfloat16),
    ]


def taps_product(wide_delta, side, x_ref, low_ref, high_ref):
    rows, hidden = x_ref.shape[:2]
    half = hidden // 2
    mine = pl.ds(pl.multiple_of(side * half, half), half)
    stack = [low_ref[mine, :]] + [x_ref[row, mine, :] for row in range(rows)] + [high_ref[mine, :]]
    wide = jnp.concatenate(stack, axis=1)
    size = rows * lanes
    parts = [
        lax.dot_general(
            wide_delta,
            wide[:, tap * lanes : tap * lanes + size],
            (((1,), (1,)), ((), ())),
            preferred_element_type=jnp.float32,
        )
        for tap in range(3)
    ]
    parts.append(jnp.zeros((padded_rows - 3 * taps_chans, half), jnp.float32))
    return jnp.concatenate(parts, axis=0)


def sent_kernel(delta_ref, x_ref, low_ref, high_ref, out_ref, spread_ref):
    pieces = []
    for row in range(x_ref.shape[0]):
        block = jnp.concatenate([delta_ref[2 * row], delta_ref[2 * row + 1]], axis=0)
        pieces.append(jnp.concatenate(spread(block), axis=0))
    wide_delta = jnp.concatenate(pieces, axis=1)
    spread_ref[...] = wide_delta
    side = 1 - lax.axis_index("rep")
    total = taps_product(wide_delta, side, x_ref, low_ref, high_ref)
    group = out_ref.shape[1]
    for block in range(out_ref.shape[0]):
        out_ref[block] = total[
            block // 2 * group : (block // 2 + 1) * group,
            block % 2 * lanes : (block % 2 + 1) * lanes,
        ].astype(jnp.bfloat16)


def kept_kernel(spread_ref, x_ref, low_ref, high_ref, other_ref, out_ref):
    side = lax.axis_index("rep")
    total = taps_product(spread_ref[...], side, x_ref, low_ref, high_ref)
    group = out_ref.shape[1]
    for block in range(out_ref.shape[0]):
        own = total[
            block // 2 * group : (block // 2 + 1) * group,
            block % 2 * lanes : (block % 2 + 1) * lanes,
        ]
        out_ref[block] = (own + other_ref[block].astype(jnp.float32)).astype(jnp.bfloat16)


def feature_grad_kernel(weight_ref, spread_ref, low_ref, high_ref, out_ref):
    rows = out_ref.shape[0]
    size = rows * lanes
    ends = []
    for ref in (low_ref, high_ref):
        block = jnp.concatenate([ref[0], ref[1]], axis=0)
        ends.append(jnp.concatenate(spread(block), axis=0))
    wide = jnp.concatenate([ends[0], spread_ref[...], ends[1]], axis=1)
    deep = jnp.concatenate(
        [wide[:, (2 - tap) * lanes : (2 - tap) * lanes + size] for tap in range(3)], axis=0
    )
    result = lax.dot_general(
        weight_ref[...], deep, (((0,), (0,)), ((), ())), preferred_element_type=jnp.float32
    )
    for row in range(rows):
        out_ref[row] = result[:, row * lanes : (row + 1) * lanes].astype(jnp.bfloat16)


def sum_kernel(scale, parts_ref, *refs):
    out_ref = refs[-1]
    total = parts_ref[0].astype(jnp.float32)
    for part in range(1, parts_ref.shape[0]):
        total = total + parts_ref[part].astype(jnp.float32)
    value = (total * scale).astype(jnp.bfloat16)
    for copy in range(out_ref.shape[0]):
        out_ref[copy] = value


def finish_kernel(away, source_ref, *refs):
    out_ref, block_ref, sem = refs[-3:]
    chans, half = block_ref.shape[1:]
    for part in range(2):
        joined = jnp.concatenate(
            [source_ref[2 * block + part] for block in range(source_ref.shape[0] // 2)], axis=0
        ).astype(jnp.float32)
        for tap in range(block_ref.shape[0]):
            block_ref[tap, :, part * lanes : (part + 1) * lanes] = joined[
                tap * padded_chans : tap * padded_chans + chans
            ]
    side = lax.axis_index("rep")
    side = 1 - side if away else side
    mine = pl.ds(pl.multiple_of(side * half, half), half)
    copy = pltpu.make_async_copy(block_ref, out_ref.at[:, :, mine], sem)
    copy.start()
    copy.wait()


vmem = pl.BlockSpec(memory_space=pltpu.VMEM)
anywhere = pl.BlockSpec(memory_space=pl.ANY)


def call(kernel, out_shape, in_specs, scratch=(), limit=32, cost=(0, 0)):
    many = isinstance(out_shape, (list, tuple))
    return pl.pallas_call(
        kernel,
        out_shape=out_shape,
        in_specs=in_specs,
        out_specs=[vmem] * len(out_shape) if many else vmem,
        scratch_shapes=list(scratch),
        cost_estimate=pl.CostEstimate(flops=cost[0], bytes_accessed=cost[1], transcendentals=0),
        compiler_params=pltpu.CompilerParams(vmem_limit_bytes=limit * 1024 * 1024),
    )


def neighbours(low_edge, high_edge):
    count = lax.axis_size("band")
    forward = [(i, i + 1) for i in range(count - 1)]
    backward = [(target, source) for source, target in forward]
    return lax.ppermute(high_edge, "band", forward), lax.ppermute(low_edge, "band", backward)


def exchange(block, axis, groups=None):
    return lax.all_to_all(block, axis, 0, 0, axis_index_groups=groups, tiled=True)


def summed(parts, copies, scale=1.0, after=()):
    return call(
        functools.partial(sum_kernel, scale),
        jax.ShapeDtypeStruct((copies,) + parts.shape[1:], jnp.bfloat16),
        [vmem] + [anywhere] * len(after),
        cost=(parts.size, 2 * parts.size),
    )(parts, *after)


def placed(away, source, shape, *before):
    return pl.pallas_call(
        functools.partial(finish_kernel, away),
        out_shape=jax.ShapeDtypeStruct(shape, jnp.float32),
        in_specs=[vmem] + [anywhere] * len(before),
        out_specs=anywhere,
        scratch_shapes=[
            pltpu.VMEM(shape[:2] + (shape[2] // 2,), jnp.float32),
            pltpu.SemaphoreType.DMA,
        ],
        input_output_aliases={1: 0} if before else {},
        cost_estimate=pl.CostEstimate(
            flops=source.size, bytes_accessed=6 * source.size, transcendentals=0
        ),
        compiler_params=pltpu.CompilerParams(vmem_limit_bytes=32 * 1024 * 1024),
    )(source, *before)


def local(features, kernel, noise_seed, noise_table, truth, area_weight):
    feature_map = features[0, 0]
    hidden, rows, cols = feature_map.shape
    chans = kernel.shape[3]
    members = lax.axis_size("member")
    place = lax.axis_index("member")
    bf16, f32 = jnp.bfloat16, jnp.float32

    x_low, x_high = neighbours(feature_map[:, 0, :], feature_map[:, rows - 1, :])
    x_rows = jnp.transpose(feature_map, (1, 0, 2))
    weights = jnp.pad(
        jnp.transpose(kernel, (0, 1, 3, 2)), ((0, 0), (0, 0), (0, padded_chans - chans), (0, 0))
    ).reshape(9 * padded_chans, hidden)
    offset = jnp.pad(
        lax.dynamic_slice(noise_table, (noise_seed[0, 0], 0), (1, chans))[0],
        (0, padded_chans - chans),
    )
    offset = jnp.broadcast_to(offset[:, None], (padded_chans, lanes))
    own_truth = jnp.pad(truth[0], ((0, padded_chans - chans), (0, 0), (0, 0)))
    own_truth = lax.dynamic_slice(
        own_truth, ((place % 2) * half_chans, place // 2, 0), (half_chans, 1, cols)
    )[:, 0, :].astype(f32)
    inner = call(
        inner_kernel,
        jax.ShapeDtypeStruct((members, half_chans, cols), f32),
        [vmem] * 3 + [anywhere],
        cost=(2 * hidden * 9 * chans * rows * cols, 4 * hidden * rows * cols),
    )(x_rows, weights, offset, own_truth)
    predicted = call(
        edge_kernel,
        jax.ShapeDtypeStruct((members, half_chans, cols), f32),
        [vmem] * 4,
        cost=(4 * hidden * 3 * chans * cols, 4 * hidden * cols),
    )(inner, x_low, x_high, weights)

    eps_value = (1.0 - alpha_level) / members
    coef = (1.0 - eps_value) / (members - 1)
    deltas = call(
        functools.partial(pair_kernel, coef),
        jax.ShapeDtypeStruct((members, half_chans, cols), bf16),
        [vmem] * 3,
        [pltpu.VMEM((members, half_chans, cols), f32)],
        cost=(members * members * 8 * half_chans * cols, 6 * members * half_chans * cols),
    )(exchange(predicted, "member"), own_truth, area_weight[None])
    delta = exchange(deltas, "member")

    d_low, d_high = neighbours(delta[:2], delta[members - 2 :])
    group = padded_rows // 8
    piece = jax.ShapeDtypeStruct((members, group, lanes), bf16)
    flops = hidden * 9 * chans * rows * cols
    sent, wide_delta = call(
        sent_kernel,
        [piece, jax.ShapeDtypeStruct((taps_chans, rows * cols), bf16)],
        [vmem] * 4,
        cost=(flops, 2 * hidden * rows * cols),
    )(delta, x_rows, x_low, x_high)
    swap = [(0, 1), (1, 0)]
    part = call(
        kept_kernel,
        piece,
        [vmem] * 5,
        cost=(flops, 2 * hidden * rows * cols),
    )(wide_delta, x_rows, x_low, x_high, lax.ppermute(sent, "rep", swap))
    grad_rows = call(
        feature_grad_kernel,
        jax.ShapeDtypeStruct((rows, hidden, cols), bf16),
        [vmem] * 4,
        cost=(2 * hidden * 9 * chans * rows * cols, 4 * hidden * rows * cols),
    )(weights, wide_delta, d_low, d_high)
    feature_grad = jnp.transpose(grad_rows, (1, 0, 2))[None, None]

    bands = lax.axis_size("band")
    near = 4
    far = bands // near
    nearby = [[far_step * near + step for step in range(near)] for far_step in range(far)]
    distant = [[far_step * near + step for far_step in range(far)] for step in range(near)]
    part = summed(exchange(part, "member"), 1)
    part = lax.all_gather(part[0], "band", axis=0, axis_index_groups=distant)
    part = summed(part, near, after=(d_low, d_high))
    scale = 1.0 / math.sqrt(lax.axis_size("rep") * members * bands * rows * cols)
    part = summed(exchange(part, "band", nearby), members, scale, after=(feature_grad,))
    part = exchange(part, "member")
    other = lax.ppermute(part, "rep", swap)
    kernel_grad = placed(False, part, (9, chans, hidden))
    kernel_grad = placed(True, other, (9, chans, hidden), kernel_grad)
    kernel_grad = jnp.transpose(kernel_grad.reshape(3, 3, chans, hidden), (0, 1, 3, 2))
    return (feature_grad, kernel_grad)


def solution(mesh):
    return jax.shard_map(
        local,
        mesh=mesh,
        in_specs=(
            P("rep", "member", None, "band", None),
            P(),
            P("rep", "member"),
            P(),
            P("rep", None, "band", None),
            P("band"),
        ),
        out_specs=(P("rep", "member", None, "band", None), P()),
        check_vma=False,
    )
```

```python
import functools
import math

import jax
import jax.numpy as jnp
from jax import lax
from jax.experimental import pallas as pl
from jax.experimental.pallas import tpu as pltpu
from jax.sharding import PartitionSpec as P

smoothing = 0.1
alpha_level = 0.95
padded_chans = 96
half_chans = padded_chans // 2
taps_chans = 3 * padded_chans
lanes = 128
padded_rows = 896


def slope(values):
    return values * lax.rsqrt(values * values + smoothing * smoothing)


def shifted(block, step):
    lane = lax.broadcasted_iota(jnp.int32, block.shape, 1)
    width = block.shape[1]
    if step == 1:
        return jnp.where(lane == 0, 0.0, pltpu.roll(block, 1, 1))
    return jnp.where(lane == width - 1, 0.0, pltpu.roll(block, width - 1, 1))


def folded(sums):
    return (
        sums[padded_chans : 2 * padded_chans]
        + shifted(sums[:padded_chans], 1)
        + shifted(sums[2 * padded_chans :], -1)
    )


def inner_kernel(x_ref, weight_ref, offset_ref, truth_ref, out_ref):
    rows = x_ref.shape[0]
    wide = jnp.concatenate([x_ref[row] for row in range(rows)], axis=1)
    sums = [
        jnp.dot(
            weight_ref[tap * taps_chans : (tap + 1) * taps_chans, :],
            wide[:, max(tap - 1, 0) * lanes : (rows + min(tap - 1, 0)) * lanes],
            preferred_element_type=jnp.float32,
        )
        for tap in range(3)
    ]
    offset = offset_ref[...]
    for row in range(rows):
        cell = sums[1][:, row * lanes : (row + 1) * lanes]
        if row > 0:
            cell = cell + sums[0][:, (row - 1) * lanes : row * lanes]
        if row < rows - 1:
            cell = cell + sums[2][:, row * lanes : (row + 1) * lanes]
        value = folded(cell) + offset
        out_ref[2 * row] = value[:half_chans]
        out_ref[2 * row + 1] = value[half_chans:]


def edge_kernel(inner_ref, low_ref, high_ref, weight_ref, out_ref):
    chunks = inner_ref.shape[0]
    for chunk in range(2, chunks - 2):
        out_ref[chunk] = inner_ref[chunk]
    for tap, ref, first in ((0, low_ref, 0), (2, high_ref, chunks - 2)):
        value = folded(
            jnp.dot(
                weight_ref[tap * taps_chans : (tap + 1) * taps_chans, :],
                ref[...],
                preferred_element_type=jnp.float32,
            )
        )
        out_ref[first] = inner_ref[first] + value[:half_chans]
        out_ref[first + 1] = inner_ref[first + 1] + value[half_chans:]


def pair_kernel(coef, values_ref, truth_ref, area_ref, out_ref, delta_ref):
    members = values_ref.shape[0]
    lane = lax.broadcasted_iota(jnp.int32, area_ref.shape, 1)
    row = lax.axis_index("member") // 2
    weight = jnp.sum(jnp.where(lane == row, area_ref[...], 0.0), axis=1, keepdims=True)
    weight = jnp.broadcast_to(weight, (8, lanes))
    for start in range(0, half_chans, 8):
        rows = slice(start, start + 8)
        values = [values_ref[member, rows, :] for member in range(members)]
        truth = truth_ref[rows, :]
        sums = [None] * members
        for one in range(members):
            for two in range(one + 1, members):
                term = slope(values[one] - values[two])
                sums[one] = term if sums[one] is None else sums[one] + term
                sums[two] = -term if sums[two] is None else sums[two] - term
        for member in range(members):
            own = slope(values[member] - truth)
            delta_ref[member, rows, :] = weight * (own - coef * sums[member])
    for member in range(members):
        out_ref[member] = delta_ref[member].astype(jnp.bfloat16)


def spread(block):
    exact = block.astype(jnp.float32)
    return [
        shifted(exact, -1).astype(jnp.bfloat16),
        block,
        shifted(exact, 1).astype(jnp.bfloat16),
    ]


def taps_product(wide_delta, side, x_ref, low_ref, high_ref):
    rows, hidden = x_ref.shape[:2]
    half = hidden // 2
    mine = pl.ds(pl.multiple_of(side * half, half), half)
    stack = [low_ref[mine, :]] + [x_ref[row, mine, :] for row in range(rows)] + [high_ref[mine, :]]
    wide = jnp.concatenate(stack, axis=1)
    size = rows * lanes
    parts = [
        lax.dot_general(
            wide_delta,
            wide[:, tap * lanes : tap * lanes + size],
            (((1,), (1,)), ((), ())),
            preferred_element_type=jnp.float32,
        )
        for tap in range(3)
    ]
    parts.append(jnp.zeros((padded_rows - 3 * taps_chans, half), jnp.float32))
    return jnp.concatenate(parts, axis=0)


def sent_kernel(delta_ref, x_ref, low_ref, high_ref, out_ref, spread_ref):
    pieces = []
    for row in range(x_ref.shape[0]):
        block = jnp.concatenate([delta_ref[2 * row], delta_ref[2 * row + 1]], axis=0)
        pieces.append(jnp.concatenate(spread(block), axis=0))
    wide_delta = jnp.concatenate(pieces, axis=1)
    spread_ref[...] = wide_delta
    side = 1 - lax.axis_index("rep")
    total = taps_product(wide_delta, side, x_ref, low_ref, high_ref)
    group = out_ref.shape[1]
    for block in range(out_ref.shape[0]):
        out_ref[block] = total[
            block // 2 * group : (block // 2 + 1) * group,
            block % 2 * lanes : (block % 2 + 1) * lanes,
        ].astype(jnp.bfloat16)


def kept_kernel(spread_ref, x_ref, low_ref, high_ref, other_ref, out_ref):
    side = lax.axis_index("rep")
    total = taps_product(spread_ref[...], side, x_ref, low_ref, high_ref)
    group = out_ref.shape[1]
    for block in range(out_ref.shape[0]):
        own = total[
            block // 2 * group : (block // 2 + 1) * group,
            block % 2 * lanes : (block % 2 + 1) * lanes,
        ]
        out_ref[block] = (own + other_ref[1 - side, block].astype(jnp.float32)).astype(jnp.bfloat16)


def feature_grad_kernel(weight_ref, spread_ref, low_ref, high_ref, out_ref):
    rows = out_ref.shape[0]
    size = rows * lanes
    ends = []
    for ref in (low_ref, high_ref):
        block = jnp.concatenate([ref[0], ref[1]], axis=0)
        ends.append(jnp.concatenate(spread(block), axis=0))
    wide = jnp.concatenate([ends[0], spread_ref[...], ends[1]], axis=1)
    deep = jnp.concatenate(
        [wide[:, (2 - tap) * lanes : (2 - tap) * lanes + size] for tap in range(3)], axis=0
    )
    result = lax.dot_general(
        weight_ref[...], deep, (((0,), (0,)), ((), ())), preferred_element_type=jnp.float32
    )
    for row in range(rows):
        out_ref[row] = result[:, row * lanes : (row + 1) * lanes].astype(jnp.bfloat16)


def sum_kernel(scale, parts_ref, *refs):
    out_ref = refs[-1]
    total = parts_ref[0].astype(jnp.float32)
    for part in range(1, parts_ref.shape[0]):
        total = total + parts_ref[part].astype(jnp.float32)
    value = (total * scale).astype(jnp.bfloat16)
    for copy in range(out_ref.shape[0]):
        out_ref[copy] = value


def finish_kernel(away, source_ref, *refs):
    out_ref, block_ref, sem = refs[-3:]
    chans, half = block_ref.shape[1:]
    for part in range(2):
        joined = jnp.concatenate(
            [source_ref[2 * block + part] for block in range(source_ref.shape[0] // 2)], axis=0
        ).astype(jnp.float32)
        for tap in range(block_ref.shape[0]):
            block_ref[tap, :, part * lanes : (part + 1) * lanes] = joined[
                tap * padded_chans : tap * padded_chans + chans
            ]
    side = lax.axis_index("rep")
    side = 1 - side if away else side
    mine = pl.ds(pl.multiple_of(side * half, half), half)
    copy = pltpu.make_async_copy(block_ref, out_ref.at[:, :, mine], sem)
    copy.start()
    copy.wait()


vmem = pl.BlockSpec(memory_space=pltpu.VMEM)
anywhere = pl.BlockSpec(memory_space=pl.ANY)


def call(kernel, out_shape, in_specs, scratch=(), limit=32, cost=(0, 0)):
    many = isinstance(out_shape, (list, tuple))
    return pl.pallas_call(
        kernel,
        out_shape=out_shape,
        in_specs=in_specs,
        out_specs=[vmem] * len(out_shape) if many else vmem,
        scratch_shapes=list(scratch),
        cost_estimate=pl.CostEstimate(flops=cost[0], bytes_accessed=cost[1], transcendentals=0),
        compiler_params=pltpu.CompilerParams(vmem_limit_bytes=limit * 1024 * 1024),
    )


def neighbours(low_edge, high_edge):
    count = lax.axis_size("band")
    forward = [(i, i + 1) for i in range(count - 1)]
    backward = [(target, source) for source, target in forward]
    return lax.ppermute(high_edge, "band", forward), lax.ppermute(low_edge, "band", backward)


def exchange(block, axis, groups=None):
    return lax.all_to_all(block, axis, 0, 0, axis_index_groups=groups, tiled=True)


def summed(parts, copies, scale=1.0, after=()):
    return call(
        functools.partial(sum_kernel, scale),
        jax.ShapeDtypeStruct((copies,) + parts.shape[1:], jnp.bfloat16),
        [vmem] + [anywhere] * len(after),
        cost=(parts.size, 2 * parts.size),
    )(parts, *after)


def placed(away, source, shape, *before):
    return pl.pallas_call(
        functools.partial(finish_kernel, away),
        out_shape=jax.ShapeDtypeStruct(shape, jnp.float32),
        in_specs=[vmem] + [anywhere] * len(before),
        out_specs=anywhere,
        scratch_shapes=[
            pltpu.VMEM(shape[:2] + (shape[2] // 2,), jnp.float32),
            pltpu.SemaphoreType.DMA,
        ],
        input_output_aliases={1: 0} if before else {},
        cost_estimate=pl.CostEstimate(
            flops=source.size, bytes_accessed=6 * source.size, transcendentals=0
        ),
        compiler_params=pltpu.CompilerParams(vmem_limit_bytes=32 * 1024 * 1024),
    )(source, *before)


def local(features, kernel, noise_seed, noise_table, truth, area_weight):
    feature_map = features[0, 0]
    hidden, rows, cols = feature_map.shape
    chans = kernel.shape[3]
    members = lax.axis_size("member")
    place = lax.axis_index("member")
    bf16, f32 = jnp.bfloat16, jnp.float32

    x_low, x_high = neighbours(feature_map[:, 0, :], feature_map[:, rows - 1, :])
    x_rows = jnp.transpose(feature_map, (1, 0, 2))
    weights = jnp.pad(
        jnp.transpose(kernel, (0, 1, 3, 2)), ((0, 0), (0, 0), (0, padded_chans - chans), (0, 0))
    ).reshape(9 * padded_chans, hidden)
    offset = jnp.pad(
        lax.dynamic_slice(noise_table, (noise_seed[0, 0], 0), (1, chans))[0],
        (0, padded_chans - chans),
    )
    offset = jnp.broadcast_to(offset[:, None], (padded_chans, lanes))
    own_truth = jnp.pad(truth[0], ((0, padded_chans - chans), (0, 0), (0, 0)))
    own_truth = lax.dynamic_slice(
        own_truth, ((place % 2) * half_chans, place // 2, 0), (half_chans, 1, cols)
    )[:, 0, :].astype(f32)
    inner = call(
        inner_kernel,
        jax.ShapeDtypeStruct((members, half_chans, cols), f32),
        [vmem] * 3 + [anywhere],
        cost=(2 * hidden * 9 * chans * rows * cols, 4 * hidden * rows * cols),
    )(x_rows, weights, offset, own_truth)
    predicted = call(
        edge_kernel,
        jax.ShapeDtypeStruct((members, half_chans, cols), f32),
        [vmem] * 4,
        cost=(4 * hidden * 3 * chans * cols, 4 * hidden * cols),
    )(inner, x_low, x_high, weights)

    eps_value = (1.0 - alpha_level) / members
    coef = (1.0 - eps_value) / (members - 1)
    deltas = call(
        functools.partial(pair_kernel, coef),
        jax.ShapeDtypeStruct((members, half_chans, cols), bf16),
        [vmem] * 3,
        [pltpu.VMEM((members, half_chans, cols), f32)],
        cost=(members * members * 8 * half_chans * cols, 6 * members * half_chans * cols),
    )(exchange(predicted, "member"), own_truth, area_weight[None])
    delta = exchange(deltas, "member")

    d_low, d_high = neighbours(delta[:2], delta[members - 2 :])
    group = padded_rows // 8
    piece = jax.ShapeDtypeStruct((members, group, lanes), bf16)
    flops = hidden * 9 * chans * rows * cols
    sent, wide_delta = call(
        sent_kernel,
        [piece, jax.ShapeDtypeStruct((taps_chans, rows * cols), bf16)],
        [vmem] * 4,
        cost=(flops, 2 * hidden * rows * cols),
    )(delta, x_rows, x_low, x_high)
    swap = [(0, 1), (1, 0)]
    part = call(
        kept_kernel,
        piece,
        [vmem] * 5,
        cost=(flops, 2 * hidden * rows * cols),
    )(wide_delta, x_rows, x_low, x_high, lax.all_gather(sent, "rep", axis=0))
    grad_rows = call(
        feature_grad_kernel,
        jax.ShapeDtypeStruct((rows, hidden, cols), bf16),
        [vmem] * 4,
        cost=(2 * hidden * 9 * chans * rows * cols, 4 * hidden * rows * cols),
    )(weights, wide_delta, d_low, d_high)
    feature_grad = jnp.transpose(grad_rows, (1, 0, 2))[None, None]

    bands = lax.axis_size("band")
    near = 4
    far = bands // near
    nearby = [[far_step * near + step for step in range(near)] for far_step in range(far)]
    distant = [[far_step * near + step for far_step in range(far)] for step in range(near)]
    def pairs(distance):
        return [
            [base + step, base + step + distance]
            for base in range(0, bands, 2 * distance)
            for step in range(distance)
        ]

    def paired(part, distance):
        return lax.all_gather(part[0], "band", axis=0, axis_index_groups=pairs(distance))

    part = summed(exchange(part, "member"), 1)
    part = summed(paired(part, 8), 1, after=(d_low, d_high))
    part = summed(paired(part, 4), near)
    scale = 1.0 / math.sqrt(lax.axis_size("rep") * members * bands * rows * cols)
    part = summed(exchange(part, "band", nearby), members, scale, after=(feature_grad,))
    part = exchange(part, "member")
    other = lax.ppermute(part, "rep", swap)
    kernel_grad = placed(False, part, (9, chans, hidden))
    kernel_grad = placed(True, other, (9, chans, hidden), kernel_grad)
    kernel_grad = jnp.transpose(kernel_grad.reshape(3, 3, chans, hidden), (0, 1, 3, 2))
    return (feature_grad, kernel_grad)


def solution(mesh):
    return jax.shard_map(
        local,
        mesh=mesh,
        in_specs=(
            P("rep", "member", None, "band", None),
            P(),
            P("rep", "member"),
            P(),
            P("rep", None, "band", None),
            P("band"),
        ),
        out_specs=(P("rep", "member", None, "band", None), P()),
        check_vma=False,
    )
```

```python
import functools
import math

import jax
import jax.numpy as jnp
from jax import lax
from jax.experimental import pallas as pl
from jax.experimental.pallas import tpu as pltpu
from jax.sharding import PartitionSpec as P

smoothing = 0.1
alpha_level = 0.95
padded_chans = 96
half_chans = padded_chans // 2
taps_chans = 3 * padded_chans
lanes = 128
padded_rows = 896


def slope(values):
    return values * lax.rsqrt(values * values + smoothing * smoothing)


def shifted(block, step):
    lane = lax.broadcasted_iota(jnp.int32, block.shape, 1)
    width = block.shape[1]
    if step == 1:
        return jnp.where(lane == 0, 0.0, pltpu.roll(block, 1, 1))
    return jnp.where(lane == width - 1, 0.0, pltpu.roll(block, width - 1, 1))


def folded(sums):
    return (
        sums[padded_chans : 2 * padded_chans]
        + shifted(sums[:padded_chans], 1)
        + shifted(sums[2 * padded_chans :], -1)
    )


def inner_kernel(x_ref, weight_ref, offset_ref, truth_ref, out_ref):
    rows = x_ref.shape[0]
    wide = jnp.concatenate([x_ref[row] for row in range(rows)], axis=1)
    sums = [
        jnp.dot(
            weight_ref[tap * taps_chans : (tap + 1) * taps_chans, :],
            wide[:, max(tap - 1, 0) * lanes : (rows + min(tap - 1, 0)) * lanes],
            preferred_element_type=jnp.float32,
        )
        for tap in range(3)
    ]
    offset = offset_ref[...]
    for row in range(rows):
        cell = sums[1][:, row * lanes : (row + 1) * lanes]
        if row > 0:
            cell = cell + sums[0][:, (row - 1) * lanes : row * lanes]
        if row < rows - 1:
            cell = cell + sums[2][:, row * lanes : (row + 1) * lanes]
        value = folded(cell) + offset
        out_ref[2 * row] = value[:half_chans]
        out_ref[2 * row + 1] = value[half_chans:]


def edge_kernel(inner_ref, high_ref, low_ref, weight_ref, out_ref):
    chunks = inner_ref.shape[0]
    for chunk in range(2, chunks - 2):
        out_ref[chunk] = inner_ref[chunk]
    for tap, ref, first in ((0, low_ref, 0), (2, high_ref, chunks - 2)):
        value = folded(
            jnp.dot(
                weight_ref[tap * taps_chans : (tap + 1) * taps_chans, :],
                ref[...],
                preferred_element_type=jnp.float32,
            )
        )
        out_ref[first] = inner_ref[first] + value[:half_chans]
        out_ref[first + 1] = inner_ref[first + 1] + value[half_chans:]


def pair_kernel(coef, values_ref, truth_ref, area_ref, out_ref, delta_ref):
    members = values_ref.shape[0]
    lane = lax.broadcasted_iota(jnp.int32, area_ref.shape, 1)
    row = lax.axis_index("member") // 2
    weight = jnp.sum(jnp.where(lane == row, area_ref[...], 0.0), axis=1, keepdims=True)
    weight = jnp.broadcast_to(weight, (8, lanes))
    for start in range(0, half_chans, 8):
        rows = slice(start, start + 8)
        values = [values_ref[member, rows, :] for member in range(members)]
        truth = truth_ref[rows, :]
        sums = [None] * members
        for one in range(members):
            for two in range(one + 1, members):
                term = slope(values[one] - values[two])
                sums[one] = term if sums[one] is None else sums[one] + term
                sums[two] = -term if sums[two] is None else sums[two] - term
        for member in range(members):
            own = slope(values[member] - truth)
            delta_ref[member, rows, :] = weight * (own - coef * sums[member])
    for member in range(members):
        out_ref[member] = delta_ref[member].astype(jnp.bfloat16)


def spread(block):
    exact = block.astype(jnp.float32)
    return [
        shifted(exact, -1).astype(jnp.bfloat16),
        block,
        shifted(exact, 1).astype(jnp.bfloat16),
    ]


def taps_product(wide_delta, side, x_ref, low_ref, high_ref):
    rows, hidden = x_ref.shape[:2]
    half = hidden // 2
    mine = pl.ds(pl.multiple_of(side * half, half), half)
    stack = [low_ref[mine, :]] + [x_ref[row, mine, :] for row in range(rows)] + [high_ref[mine, :]]
    wide = jnp.concatenate(stack, axis=1)
    size = rows * lanes
    parts = [
        lax.dot_general(
            wide_delta,
            wide[:, tap * lanes : tap * lanes + size],
            (((1,), (1,)), ((), ())),
            preferred_element_type=jnp.float32,
        )
        for tap in range(3)
    ]
    parts.append(jnp.zeros((padded_rows - 3 * taps_chans, half), jnp.float32))
    return jnp.concatenate(parts, axis=0)


def sent_kernel(delta_ref, x_ref, high_ref, low_ref, out_ref, spread_ref):
    pieces = []
    for row in range(x_ref.shape[0]):
        block = jnp.concatenate([delta_ref[2 * row], delta_ref[2 * row + 1]], axis=0)
        pieces.append(jnp.concatenate(spread(block), axis=0))
    wide_delta = jnp.concatenate(pieces, axis=1)
    spread_ref[...] = wide_delta
    side = 1 - lax.axis_index("rep")
    total = taps_product(wide_delta, side, x_ref, low_ref, high_ref)
    group = out_ref.shape[1]
    for block in range(out_ref.shape[0]):
        out_ref[block] = total[
            block // 2 * group : (block // 2 + 1) * group,
            block % 2 * lanes : (block % 2 + 1) * lanes,
        ].astype(jnp.bfloat16)


def kept_kernel(spread_ref, x_ref, high_ref, low_ref, other_ref, out_ref):
    side = lax.axis_index("rep")
    total = taps_product(spread_ref[...], side, x_ref, low_ref, high_ref)
    group = out_ref.shape[1]
    for block in range(out_ref.shape[0]):
        own = total[
            block // 2 * group : (block // 2 + 1) * group,
            block % 2 * lanes : (block % 2 + 1) * lanes,
        ]
        out_ref[block] = (own + other_ref[1 - side, block].astype(jnp.float32)).astype(jnp.bfloat16)


def feature_grad_kernel(weight_ref, spread_ref, high_ref, low_ref, out_ref):
    rows = out_ref.shape[0]
    size = rows * lanes
    ends = []
    for ref in (low_ref, high_ref):
        block = jnp.concatenate([ref[0], ref[1]], axis=0)
        ends.append(jnp.concatenate(spread(block), axis=0))
    wide = jnp.concatenate([ends[0], spread_ref[...], ends[1]], axis=1)
    deep = jnp.concatenate(
        [wide[:, (2 - tap) * lanes : (2 - tap) * lanes + size] for tap in range(3)], axis=0
    )
    result = lax.dot_general(
        weight_ref[...], deep, (((0,), (0,)), ((), ())), preferred_element_type=jnp.float32
    )
    for row in range(rows):
        out_ref[row] = result[:, row * lanes : (row + 1) * lanes].astype(jnp.bfloat16)


def sum_kernel(scale, parts_ref, *refs):
    out_ref = refs[-1]
    total = parts_ref[0].astype(jnp.float32)
    for part in range(1, parts_ref.shape[0]):
        total = total + parts_ref[part].astype(jnp.float32)
    value = (total * scale).astype(jnp.bfloat16)
    for copy in range(out_ref.shape[0]):
        out_ref[copy] = value


def finish_kernel(source_ref, out_ref, block_ref, sems):
    sides, chunks = source_ref.shape[:2]
    taps, chans = block_ref.shape[1:3]
    half = block_ref.shape[3]
    copies = []
    for side in range(sides):
        for part in range(2):
            joined = jnp.concatenate(
                [source_ref[side, 2 * block + part] for block in range(chunks // 2)], axis=0
            ).astype(jnp.float32)
            for tap in range(taps):
                block_ref[side, tap, :, part * lanes : (part + 1) * lanes] = joined[
                    tap * padded_chans : tap * padded_chans + chans
                ]
        copies.append(
            pltpu.make_async_copy(
                block_ref.at[side],
                out_ref.at[:, :, pl.ds(side * half, half)],
                sems.at[side],
            )
        )
        copies[-1].start()
    for copy in copies:
        copy.wait()


vmem = pl.BlockSpec(memory_space=pltpu.VMEM)
anywhere = pl.BlockSpec(memory_space=pl.ANY)


def call(kernel, out_shape, in_specs, scratch=(), limit=32, cost=(0, 0)):
    many = isinstance(out_shape, (list, tuple))
    return pl.pallas_call(
        kernel,
        out_shape=out_shape,
        in_specs=in_specs,
        out_specs=[vmem] * len(out_shape) if many else vmem,
        scratch_shapes=list(scratch),
        cost_estimate=pl.CostEstimate(flops=cost[0], bytes_accessed=cost[1], transcendentals=0),
        compiler_params=pltpu.CompilerParams(vmem_limit_bytes=limit * 1024 * 1024),
    )


def neighbours(low_edge, high_edge):
    count = lax.axis_size("band")
    forward = [(i, i + 1) for i in range(count - 1)]
    backward = [(target, source) for source, target in forward]
    return lax.ppermute(high_edge, "band", forward), lax.ppermute(low_edge, "band", backward)


def exchange(block, axis, groups=None):
    return lax.all_to_all(block, axis, 0, 0, axis_index_groups=groups, tiled=True)


def summed(parts, copies, scale=1.0, after=()):
    return call(
        functools.partial(sum_kernel, scale),
        jax.ShapeDtypeStruct((copies,) + parts.shape[1:], jnp.bfloat16),
        [vmem] + [anywhere] * len(after),
        cost=(parts.size, 2 * parts.size),
    )(parts, *after)


def placed(source, shape):
    sides = source.shape[0]
    return pl.pallas_call(
        finish_kernel,
        out_shape=jax.ShapeDtypeStruct(shape, jnp.float32),
        in_specs=[vmem],
        out_specs=anywhere,
        scratch_shapes=[
            pltpu.VMEM((sides,) + shape[:2] + (shape[2] // sides,), jnp.float32),
            pltpu.SemaphoreType.DMA((sides,)),
        ],
        cost_estimate=pl.CostEstimate(
            flops=source.size, bytes_accessed=6 * source.size, transcendentals=0
        ),
        compiler_params=pltpu.CompilerParams(vmem_limit_bytes=32 * 1024 * 1024),
    )(source)


def local(features, kernel, noise_seed, noise_table, truth, area_weight):
    feature_map = features[0, 0]
    hidden, rows, cols = feature_map.shape
    chans = kernel.shape[3]
    members = lax.axis_size("member")
    place = lax.axis_index("member")
    bf16, f32 = jnp.bfloat16, jnp.float32

    x_low, x_high = neighbours(feature_map[:, 0, :], feature_map[:, rows - 1, :])
    x_rows = jnp.transpose(feature_map, (1, 0, 2))
    weights = jnp.pad(
        jnp.transpose(kernel, (0, 1, 3, 2)), ((0, 0), (0, 0), (0, padded_chans - chans), (0, 0))
    ).reshape(9 * padded_chans, hidden)
    offset = jnp.pad(
        lax.dynamic_slice(noise_table, (noise_seed[0, 0], 0), (1, chans))[0],
        (0, padded_chans - chans),
    )
    offset = jnp.broadcast_to(offset[:, None], (padded_chans, lanes))
    own_truth = jnp.pad(truth[0], ((0, padded_chans - chans), (0, 0), (0, 0)))
    own_truth = lax.dynamic_slice(
        own_truth, ((place % 2) * half_chans, place // 2, 0), (half_chans, 1, cols)
    )[:, 0, :].astype(f32)
    inner = call(
        inner_kernel,
        jax.ShapeDtypeStruct((members, half_chans, cols), f32),
        [vmem] * 3 + [anywhere],
        cost=(2 * hidden * 9 * chans * rows * cols, 4 * hidden * rows * cols),
    )(x_rows, weights, offset, own_truth)
    predicted = call(
        edge_kernel,
        jax.ShapeDtypeStruct((members, half_chans, cols), f32),
        [vmem] * 4,
        cost=(4 * hidden * 3 * chans * cols, 4 * hidden * cols),
    )(inner, x_high, x_low, weights)

    eps_value = (1.0 - alpha_level) / members
    coef = (1.0 - eps_value) / (members - 1)
    deltas = call(
        functools.partial(pair_kernel, coef),
        jax.ShapeDtypeStruct((members, half_chans, cols), bf16),
        [vmem] * 3,
        [pltpu.VMEM((members, half_chans, cols), f32)],
        cost=(members * members * 8 * half_chans * cols, 6 * members * half_chans * cols),
    )(exchange(predicted, "member"), own_truth, area_weight[None])
    delta = exchange(deltas, "member")

    d_low, d_high = neighbours(delta[:2], delta[members - 2 :])
    group = padded_rows // 8
    piece = jax.ShapeDtypeStruct((members, group, lanes), bf16)
    flops = hidden * 9 * chans * rows * cols
    sent, wide_delta = call(
        sent_kernel,
        [piece, jax.ShapeDtypeStruct((taps_chans, rows * cols), bf16)],
        [vmem] * 4,
        cost=(flops, 2 * hidden * rows * cols),
    )(delta, x_rows, x_high, x_low)
    part = call(
        kept_kernel,
        piece,
        [vmem] * 5,
        cost=(flops, 2 * hidden * rows * cols),
    )(wide_delta, x_rows, x_high, x_low, lax.all_gather(sent, "rep", axis=0))
    grad_rows = call(
        feature_grad_kernel,
        jax.ShapeDtypeStruct((rows, hidden, cols), bf16),
        [vmem] * 4,
        cost=(2 * hidden * 9 * chans * rows * cols, 4 * hidden * rows * cols),
    )(weights, wide_delta, d_high, d_low)
    feature_grad = jnp.transpose(grad_rows, (1, 0, 2))[None, None]

    bands = lax.axis_size("band")
    near = 4
    far = bands // near
    nearby = [[far_step * near + step for step in range(near)] for far_step in range(far)]
    distant = [[far_step * near + step for far_step in range(far)] for step in range(near)]
    def pairs(distance):
        return [
            [base + step, base + step + distance]
            for base in range(0, bands, 2 * distance)
            for step in range(distance)
        ]

    def paired(part, distance):
        return lax.all_gather(part[0], "band", axis=0, axis_index_groups=pairs(distance))

    part = summed(exchange(part, "member"), 1)
    part = summed(paired(part, 8), 1, after=(d_high, d_low))
    part = summed(paired(part, 4), near)
    scale = 1.0 / math.sqrt(lax.axis_size("rep") * members * bands * rows * cols)
    part = summed(exchange(part, "band", nearby), members, scale, after=(feature_grad,))
    part = exchange(part, "member")
    kernel_grad = placed(lax.all_gather(part, "rep", axis=0), (9, chans, hidden))
    kernel_grad = jnp.transpose(kernel_grad.reshape(3, 3, chans, hidden), (0, 1, 3, 2))
    return (feature_grad, kernel_grad)


def solution(mesh):
    return jax.shard_map(
        local,
        mesh=mesh,
        in_specs=(
            P("rep", "member", None, "band", None),
            P(),
            P("rep", "member"),
            P(),
            P("rep", None, "band", None),
            P("band"),
        ),
        out_specs=(P("rep", "member", None, "band", None), P()),
        check_vma=False,
    )
```

```python
import functools
import math

import jax
import jax.numpy as jnp
from jax import lax
from jax.experimental import pallas as pl
from jax.experimental.pallas import tpu as pltpu
from jax.sharding import PartitionSpec as P

smoothing = 0.1
alpha_level = 0.95
padded_chans = 96
half_chans = padded_chans // 2
taps_chans = 3 * padded_chans
lanes = 128
padded_rows = 896


def slope(values):
    return values * lax.rsqrt(values * values + smoothing * smoothing)


def shifted(block, step):
    lane = lax.broadcasted_iota(jnp.int32, block.shape, 1)
    width = block.shape[1]
    if step == 1:
        return jnp.where(lane == 0, 0.0, pltpu.roll(block, 1, 1))
    return jnp.where(lane == width - 1, 0.0, pltpu.roll(block, width - 1, 1))


def folded(sums):
    return (
        sums[padded_chans : 2 * padded_chans]
        + shifted(sums[:padded_chans], 1)
        + shifted(sums[2 * padded_chans :], -1)
    )


def inner_kernel(x_ref, weight_ref, offset_ref, truth_ref, out_ref):
    rows = x_ref.shape[0]
    wide = jnp.concatenate([x_ref[row] for row in range(rows)], axis=1)
    sums = [
        jnp.dot(
            weight_ref[tap * taps_chans : (tap + 1) * taps_chans, :],
            wide[:, max(tap - 1, 0) * lanes : (rows + min(tap - 1, 0)) * lanes],
            preferred_element_type=jnp.float32,
        )
        for tap in range(3)
    ]
    offset = offset_ref[...]
    for row in range(rows):
        cell = sums[1][:, row * lanes : (row + 1) * lanes]
        if row > 0:
            cell = cell + sums[0][:, (row - 1) * lanes : row * lanes]
        if row < rows - 1:
            cell = cell + sums[2][:, row * lanes : (row + 1) * lanes]
        value = folded(cell) + offset
        out_ref[2 * row] = value[:half_chans]
        out_ref[2 * row + 1] = value[half_chans:]


def edge_kernel(inner_ref, high_ref, low_ref, weight_ref, out_ref):
    chunks = inner_ref.shape[0]
    for chunk in range(2, chunks - 2):
        out_ref[chunk] = inner_ref[chunk]
    for tap, ref, first in ((0, low_ref, 0), (2, high_ref, chunks - 2)):
        value = folded(
            jnp.dot(
                weight_ref[tap * taps_chans : (tap + 1) * taps_chans, :],
                ref[...],
                preferred_element_type=jnp.float32,
            )
        )
        out_ref[first] = inner_ref[first] + value[:half_chans]
        out_ref[first + 1] = inner_ref[first + 1] + value[half_chans:]


def pair_kernel(coef, values_ref, truth_ref, area_ref, out_ref, delta_ref):
    members = values_ref.shape[0]
    lane = lax.broadcasted_iota(jnp.int32, area_ref.shape, 1)
    row = lax.axis_index("member") // 2
    weight = jnp.sum(jnp.where(lane == row, area_ref[...], 0.0), axis=1, keepdims=True)
    weight = jnp.broadcast_to(weight, (8, lanes))
    for start in range(0, half_chans, 8):
        rows = slice(start, start + 8)
        values = [values_ref[member, rows, :] for member in range(members)]
        truth = truth_ref[rows, :]
        sums = [None] * members
        for one in range(members):
            for two in range(one + 1, members):
                term = slope(values[one] - values[two])
                sums[one] = term if sums[one] is None else sums[one] + term
                sums[two] = -term if sums[two] is None else sums[two] - term
        for member in range(members):
            own = slope(values[member] - truth)
            delta_ref[member, rows, :] = weight * (own - coef * sums[member])
    for member in range(members):
        out_ref[member] = delta_ref[member].astype(jnp.bfloat16)


def spread(block):
    exact = block.astype(jnp.float32)
    return [
        shifted(exact, -1).astype(jnp.bfloat16),
        block,
        shifted(exact, 1).astype(jnp.bfloat16),
    ]


def taps_product(wide_delta, side, x_ref, low_ref, high_ref):
    rows, hidden = x_ref.shape[:2]
    half = hidden // 2
    mine = pl.ds(pl.multiple_of(side * half, half), half)
    stack = [low_ref[mine, :]] + [x_ref[row, mine, :] for row in range(rows)] + [high_ref[mine, :]]
    wide = jnp.concatenate(stack, axis=1)
    size = rows * lanes
    parts = [
        lax.dot_general(
            wide_delta,
            wide[:, tap * lanes : tap * lanes + size],
            (((1,), (1,)), ((), ())),
            preferred_element_type=jnp.float32,
        )
        for tap in range(3)
    ]
    parts.append(jnp.zeros((padded_rows - 3 * taps_chans, half), jnp.float32))
    return jnp.concatenate(parts, axis=0)


def sent_kernel(delta_ref, x_ref, high_ref, low_ref, out_ref, spread_ref):
    pieces = []
    for row in range(x_ref.shape[0]):
        block = jnp.concatenate([delta_ref[2 * row], delta_ref[2 * row + 1]], axis=0)
        pieces.append(jnp.concatenate(spread(block), axis=0))
    wide_delta = jnp.concatenate(pieces, axis=1)
    spread_ref[...] = wide_delta
    side = 1 - lax.axis_index("rep")
    total = taps_product(wide_delta, side, x_ref, low_ref, high_ref)
    group = out_ref.shape[1]
    for block in range(out_ref.shape[0]):
        out_ref[block] = total[
            block // 2 * group : (block // 2 + 1) * group,
            block % 2 * lanes : (block % 2 + 1) * lanes,
        ].astype(jnp.bfloat16)


def kept_kernel(spread_ref, x_ref, high_ref, low_ref, other_ref, out_ref):
    side = lax.axis_index("rep")
    total = taps_product(spread_ref[...], side, x_ref, low_ref, high_ref)
    group = out_ref.shape[1]
    for block in range(out_ref.shape[0]):
        own = total[
            block // 2 * group : (block // 2 + 1) * group,
            block % 2 * lanes : (block % 2 + 1) * lanes,
        ]
        out_ref[block] = (own + other_ref[1 - side, block].astype(jnp.float32)).astype(jnp.bfloat16)


def feature_grad_kernel(weight_ref, spread_ref, high_ref, low_ref, out_ref):
    rows = out_ref.shape[0]
    size = rows * lanes
    ends = []
    for ref in (low_ref, high_ref):
        block = jnp.concatenate([ref[0], ref[1]], axis=0)
        ends.append(jnp.concatenate(spread(block), axis=0))
    wide = jnp.concatenate([ends[0], spread_ref[...], ends[1]], axis=1)
    deep = jnp.concatenate(
        [wide[:, (2 - tap) * lanes : (2 - tap) * lanes + size] for tap in range(3)], axis=0
    )
    result = lax.dot_general(
        weight_ref[...], deep, (((0,), (0,)), ((), ())), preferred_element_type=jnp.float32
    )
    for row in range(rows):
        out_ref[row] = result[:, row * lanes : (row + 1) * lanes].astype(jnp.bfloat16)


def sum_kernel(scale, parts_ref, *refs):
    out_ref = refs[-1]
    total = parts_ref[0].astype(jnp.float32)
    for part in range(1, parts_ref.shape[0]):
        total = total + parts_ref[part].astype(jnp.float32)
    value = (total * scale).astype(jnp.bfloat16)
    for copy in range(out_ref.shape[0]):
        out_ref[copy] = value


def finish_kernel(source_ref, out_ref, block_ref, sems):
    sides, chunks = source_ref.shape[:2]
    taps, chans = block_ref.shape[1:3]
    half = block_ref.shape[3]
    copies = []
    for side in range(sides):
        for part in range(2):
            joined = jnp.concatenate(
                [source_ref[side, 2 * block + part] for block in range(chunks // 2)], axis=0
            ).astype(jnp.float32)
            for tap in range(taps):
                block_ref[side, tap, :, part * lanes : (part + 1) * lanes] = joined[
                    tap * padded_chans : tap * padded_chans + chans
                ]
        copies.append(
            pltpu.make_async_copy(
                block_ref.at[side],
                out_ref.at[:, :, pl.ds(side * half, half)],
                sems.at[side],
            )
        )
        copies[-1].start()
    for copy in copies:
        copy.wait()


vmem = pl.BlockSpec(memory_space=pltpu.VMEM)
anywhere = pl.BlockSpec(memory_space=pl.ANY)


def call(kernel, out_shape, in_specs, scratch=(), limit=32, cost=(0, 0)):
    many = isinstance(out_shape, (list, tuple))
    return pl.pallas_call(
        kernel,
        out_shape=out_shape,
        in_specs=in_specs,
        out_specs=[vmem] * len(out_shape) if many else vmem,
        scratch_shapes=list(scratch),
        cost_estimate=pl.CostEstimate(flops=cost[0], bytes_accessed=cost[1], transcendentals=0),
        compiler_params=pltpu.CompilerParams(vmem_limit_bytes=limit * 1024 * 1024),
    )


def neighbours(low_edge, high_edge):
    count = lax.axis_size("band")
    forward = [(i, i + 1) for i in range(count - 1)]
    backward = [(target, source) for source, target in forward]
    return lax.ppermute(high_edge, "band", forward), lax.ppermute(low_edge, "band", backward)


def exchange(block, axis, groups=None):
    return lax.all_to_all(block, axis, 0, 0, axis_index_groups=groups, tiled=True)


def summed(parts, copies, scale=1.0, after=()):
    return call(
        functools.partial(sum_kernel, scale),
        jax.ShapeDtypeStruct((copies,) + parts.shape[1:], jnp.bfloat16),
        [vmem] + [anywhere] * len(after),
        cost=(parts.size, 2 * parts.size),
    )(parts, *after)


def placed(source, shape):
    sides = source.shape[0]
    return pl.pallas_call(
        finish_kernel,
        out_shape=jax.ShapeDtypeStruct(shape, jnp.float32),
        in_specs=[vmem],
        out_specs=anywhere,
        scratch_shapes=[
            pltpu.VMEM((sides,) + shape[:2] + (shape[2] // sides,), jnp.float32),
            pltpu.SemaphoreType.DMA((sides,)),
        ],
        cost_estimate=pl.CostEstimate(
            flops=source.size, bytes_accessed=6 * source.size, transcendentals=0
        ),
        compiler_params=pltpu.CompilerParams(vmem_limit_bytes=32 * 1024 * 1024),
    )(source)


def local(features, kernel, noise_seed, noise_table, truth, area_weight):
    feature_map = features[0, 0]
    hidden, rows, cols = feature_map.shape
    chans = kernel.shape[3]
    members = lax.axis_size("member")
    place = lax.axis_index("member")
    bf16, f32 = jnp.bfloat16, jnp.float32

    x_low, x_high = neighbours(feature_map[:, 0, :], feature_map[:, rows - 1, :])
    x_rows = jnp.transpose(feature_map, (1, 0, 2))
    weights = jnp.pad(
        jnp.transpose(kernel, (0, 1, 3, 2)), ((0, 0), (0, 0), (0, padded_chans - chans), (0, 0))
    ).reshape(9 * padded_chans, hidden)
    offset = jnp.pad(
        lax.dynamic_slice(noise_table, (noise_seed[0, 0], 0), (1, chans))[0],
        (0, padded_chans - chans),
    )
    offset = jnp.broadcast_to(offset[:, None], (padded_chans, lanes))
    own_truth = jnp.pad(truth[0], ((0, padded_chans - chans), (0, 0), (0, 0)))
    own_truth = lax.dynamic_slice(
        own_truth, ((place % 2) * half_chans, place // 2, 0), (half_chans, 1, cols)
    )[:, 0, :].astype(f32)
    inner = call(
        inner_kernel,
        jax.ShapeDtypeStruct((members, half_chans, cols), f32),
        [vmem] * 3 + [anywhere],
        cost=(2 * hidden * 9 * chans * rows * cols, 4 * hidden * rows * cols),
    )(x_rows, weights, offset, own_truth)
    predicted = call(
        edge_kernel,
        jax.ShapeDtypeStruct((members, half_chans, cols), f32),
        [vmem] * 4,
        cost=(4 * hidden * 3 * chans * cols, 4 * hidden * cols),
    )(inner, x_high, x_low, weights)

    eps_value = (1.0 - alpha_level) / members
    coef = (1.0 - eps_value) / (members - 1)
    deltas = call(
        functools.partial(pair_kernel, coef),
        jax.ShapeDtypeStruct((members, half_chans, cols), bf16),
        [vmem] * 3,
        [pltpu.VMEM((members, half_chans, cols), f32)],
        cost=(members * members * 8 * half_chans * cols, 6 * members * half_chans * cols),
    )(exchange(predicted, "member"), own_truth, area_weight[None])
    delta = exchange(deltas, "member")

    d_low, d_high = neighbours(delta[:2], delta[members - 2 :])
    group = padded_rows // 8
    piece = jax.ShapeDtypeStruct((members, group, lanes), bf16)
    flops = hidden * 9 * chans * rows * cols
    sent, wide_delta = call(
        sent_kernel,
        [piece, jax.ShapeDtypeStruct((taps_chans, rows * cols), bf16)],
        [vmem] * 4,
        cost=(flops, 2 * hidden * rows * cols),
    )(delta, x_rows, x_high, x_low)
    part = call(
        kept_kernel,
        piece,
        [vmem] * 5,
        cost=(flops, 2 * hidden * rows * cols),
    )(wide_delta, x_rows, x_high, x_low, lax.all_gather(sent, "rep", axis=0))
    grad_rows = call(
        feature_grad_kernel,
        jax.ShapeDtypeStruct((rows, hidden, cols), bf16),
        [vmem] * 4,
        cost=(2 * hidden * 9 * chans * rows * cols, 4 * hidden * rows * cols),
    )(weights, wide_delta, d_high, d_low)
    feature_grad = jnp.transpose(grad_rows, (1, 0, 2))[None, None]

    bands = lax.axis_size("band")
    near = 4
    far = bands // near
    nearby = [[far_step * near + step for step in range(near)] for far_step in range(far)]
    distant = [[far_step * near + step for far_step in range(far)] for step in range(near)]
    def pairs(distance):
        return [
            [base + step, base + step + distance]
            for base in range(0, bands, 2 * distance)
            for step in range(distance)
        ]

    def paired(part, distance):
        return lax.all_gather(part[0], "band", axis=0, axis_index_groups=pairs(distance))

    part = summed(exchange(part, "member"), 1)
    part = summed(paired(part, 4), 1, after=(d_high, d_low))
    part = summed(paired(part, 8), near)
    scale = 1.0 / math.sqrt(lax.axis_size("rep") * members * bands * rows * cols)
    part = summed(exchange(part, "band", nearby), members, scale, after=(feature_grad,))
    part = exchange(part, "member")
    kernel_grad = placed(lax.all_gather(part, "rep", axis=0), (9, chans, hidden))
    kernel_grad = jnp.transpose(kernel_grad.reshape(3, 3, chans, hidden), (0, 1, 3, 2))
    return (feature_grad, kernel_grad)


def solution(mesh):
    return jax.shard_map(
        local,
        mesh=mesh,
        in_specs=(
            P("rep", "member", None, "band", None),
            P(),
            P("rep", "member"),
            P(),
            P("rep", None, "band", None),
            P("band"),
        ),
        out_specs=(P("rep", "member", None, "band", None), P()),
        check_vma=False,
    )
```

```python
import functools
import math

import jax
import jax.numpy as jnp
from jax import lax
from jax.experimental import pallas as pl
from jax.experimental.pallas import tpu as pltpu
from jax.sharding import PartitionSpec as P

smoothing = 0.1
alpha_level = 0.95
padded_chans = 96
half_chans = padded_chans // 2
taps_chans = 3 * padded_chans
lanes = 128
padded_rows = 896


def slope(values):
    return values * lax.rsqrt(values * values + smoothing * smoothing)


def shifted(block, step):
    lane = lax.broadcasted_iota(jnp.int32, block.shape, 1)
    width = block.shape[1]
    if step == 1:
        return jnp.where(lane == 0, 0.0, pltpu.roll(block, 1, 1))
    return jnp.where(lane == width - 1, 0.0, pltpu.roll(block, width - 1, 1))


def folded(sums):
    return (
        sums[padded_chans : 2 * padded_chans]
        + shifted(sums[:padded_chans], 1)
        + shifted(sums[2 * padded_chans :], -1)
    )


def inner_kernel(x_ref, weight_ref, offset_ref, truth_ref, out_ref):
    rows = x_ref.shape[0]
    wide = jnp.concatenate([x_ref[row] for row in range(rows)], axis=1)
    sums = [
        jnp.dot(
            weight_ref[tap * taps_chans : (tap + 1) * taps_chans, :],
            wide[:, max(tap - 1, 0) * lanes : (rows + min(tap - 1, 0)) * lanes],
            preferred_element_type=jnp.float32,
        )
        for tap in range(3)
    ]
    offset = offset_ref[...]
    for row in range(rows):
        cell = sums[1][:, row * lanes : (row + 1) * lanes]
        if row > 0:
            cell = cell + sums[0][:, (row - 1) * lanes : row * lanes]
        if row < rows - 1:
            cell = cell + sums[2][:, row * lanes : (row + 1) * lanes]
        value = folded(cell) + offset
        out_ref[2 * row] = value[:half_chans]
        out_ref[2 * row + 1] = value[half_chans:]


def edge_kernel(inner_ref, high_ref, low_ref, weight_ref, out_ref):
    chunks = inner_ref.shape[0]
    for chunk in range(2, chunks - 2):
        out_ref[chunk] = inner_ref[chunk]
    for tap, ref, first in ((0, low_ref, 0), (2, high_ref, chunks - 2)):
        value = folded(
            jnp.dot(
                weight_ref[tap * taps_chans : (tap + 1) * taps_chans, :],
                ref[...],
                preferred_element_type=jnp.float32,
            )
        )
        out_ref[first] = inner_ref[first] + value[:half_chans]
        out_ref[first + 1] = inner_ref[first + 1] + value[half_chans:]


def pair_kernel(coef, values_ref, truth_ref, area_ref, out_ref, delta_ref):
    members = values_ref.shape[0]
    lane = lax.broadcasted_iota(jnp.int32, area_ref.shape, 1)
    row = lax.axis_index("member") // 2
    weight = jnp.sum(jnp.where(lane == row, area_ref[...], 0.0), axis=1, keepdims=True)
    weight = jnp.broadcast_to(weight, (8, lanes))
    for start in range(0, half_chans, 8):
        rows = slice(start, start + 8)
        values = [values_ref[member, rows, :] for member in range(members)]
        truth = truth_ref[rows, :]
        sums = [None] * members
        for one in range(members):
            for two in range(one + 1, members):
                term = slope(values[one] - values[two])
                sums[one] = term if sums[one] is None else sums[one] + term
                sums[two] = -term if sums[two] is None else sums[two] - term
        for member in range(members):
            own = slope(values[member] - truth)
            delta_ref[member, rows, :] = weight * (own - coef * sums[member])
    for member in range(members):
        out_ref[member] = delta_ref[member].astype(jnp.bfloat16)


def spread(block):
    exact = block.astype(jnp.float32)
    return [
        shifted(exact, -1).astype(jnp.bfloat16),
        block,
        shifted(exact, 1).astype(jnp.bfloat16),
    ]


def taps_product(wide_delta, side, x_ref, low_ref, high_ref):
    rows, hidden = x_ref.shape[:2]
    half = hidden // 2
    mine = pl.ds(pl.multiple_of(side * half, half), half)
    stack = [low_ref[mine, :]] + [x_ref[row, mine, :] for row in range(rows)] + [high_ref[mine, :]]
    wide = jnp.concatenate(stack, axis=1)
    size = rows * lanes
    parts = [
        lax.dot_general(
            wide_delta,
            wide[:, tap * lanes : tap * lanes + size],
            (((1,), (1,)), ((), ())),
            preferred_element_type=jnp.float32,
        )
        for tap in range(3)
    ]
    parts.append(jnp.zeros((padded_rows - 3 * taps_chans, half), jnp.float32))
    return jnp.concatenate(parts, axis=0)


def sent_kernel(delta_ref, x_ref, high_ref, low_ref, out_ref, spread_ref):
    pieces = []
    for row in range(x_ref.shape[0]):
        block = jnp.concatenate([delta_ref[2 * row], delta_ref[2 * row + 1]], axis=0)
        pieces.append(jnp.concatenate(spread(block), axis=0))
    wide_delta = jnp.concatenate(pieces, axis=1)
    spread_ref[...] = wide_delta
    side = 1 - lax.axis_index("rep")
    total = taps_product(wide_delta, side, x_ref, low_ref, high_ref)
    group = out_ref.shape[1]
    for block in range(out_ref.shape[0]):
        out_ref[block] = total[
            block // 2 * group : (block // 2 + 1) * group,
            block % 2 * lanes : (block % 2 + 1) * lanes,
        ].astype(jnp.bfloat16)


def kept_kernel(spread_ref, x_ref, high_ref, low_ref, other_ref, out_ref):
    side = lax.axis_index("rep")
    total = taps_product(spread_ref[...], side, x_ref, low_ref, high_ref)
    group = out_ref.shape[1]
    for block in range(out_ref.shape[0]):
        own = total[
            block // 2 * group : (block // 2 + 1) * group,
            block % 2 * lanes : (block % 2 + 1) * lanes,
        ]
        out_ref[block] = (own + other_ref[1 - side, block].astype(jnp.float32)).astype(jnp.bfloat16)


def feature_grad_kernel(weight_ref, spread_ref, high_ref, low_ref, out_ref):
    rows = out_ref.shape[0]
    size = rows * lanes
    ends = []
    for ref in (low_ref, high_ref):
        block = jnp.concatenate([ref[0], ref[1]], axis=0)
        ends.append(jnp.concatenate(spread(block), axis=0))
    wide = jnp.concatenate([ends[0], spread_ref[...], ends[1]], axis=1)
    deep = jnp.concatenate(
        [wide[:, (2 - tap) * lanes : (2 - tap) * lanes + size] for tap in range(3)], axis=0
    )
    result = lax.dot_general(
        weight_ref[...], deep, (((0,), (0,)), ((), ())), preferred_element_type=jnp.float32
    )
    for row in range(rows):
        out_ref[row] = result[:, row * lanes : (row + 1) * lanes].astype(jnp.bfloat16)


def sum_kernel(scale, parts_ref, *refs):
    out_ref = refs[-1]
    total = parts_ref[0].astype(jnp.float32)
    for part in range(1, parts_ref.shape[0]):
        total = total + parts_ref[part].astype(jnp.float32)
    value = (total * scale).astype(jnp.bfloat16)
    for copy in range(out_ref.shape[0]):
        out_ref[copy] = value


def finish_kernel(source_ref, out_ref, block_ref, sems):
    sides, chunks = source_ref.shape[:2]
    taps, chans = block_ref.shape[1:3]
    half = block_ref.shape[3]
    copies = []
    for side in range(sides):
        for part in range(2):
            joined = jnp.concatenate(
                [source_ref[side, 2 * block + part] for block in range(chunks // 2)], axis=0
            ).astype(jnp.float32)
            for tap in range(taps):
                block_ref[side, tap, :, part * lanes : (part + 1) * lanes] = joined[
                    tap * padded_chans : tap * padded_chans + chans
                ]
        copies.append(
            pltpu.make_async_copy(
                block_ref.at[side],
                out_ref.at[:, :, pl.ds(side * half, half)],
                sems.at[side],
            )
        )
        copies[-1].start()
    for copy in copies:
        copy.wait()


vmem = pl.BlockSpec(memory_space=pltpu.VMEM)
anywhere = pl.BlockSpec(memory_space=pl.ANY)


def call(kernel, out_shape, in_specs, scratch=(), limit=14, cost=(0, 0)):
    many = isinstance(out_shape, (list, tuple))
    return pl.pallas_call(
        kernel,
        out_shape=out_shape,
        in_specs=in_specs,
        out_specs=[vmem] * len(out_shape) if many else vmem,
        scratch_shapes=list(scratch),
        cost_estimate=pl.CostEstimate(flops=cost[0], bytes_accessed=cost[1], transcendentals=0),
        compiler_params=pltpu.CompilerParams(vmem_limit_bytes=limit * 1024 * 1024),
    )


def neighbours(low_edge, high_edge):
    count = lax.axis_size("band")
    forward = [(i, i + 1) for i in range(count - 1)]
    backward = [(target, source) for source, target in forward]
    return lax.ppermute(high_edge, "band", forward), lax.ppermute(low_edge, "band", backward)


def exchange(block, axis, groups=None):
    return lax.all_to_all(block, axis, 0, 0, axis_index_groups=groups, tiled=True)


def summed(parts, copies, scale=1.0, after=()):
    return call(
        functools.partial(sum_kernel, scale),
        jax.ShapeDtypeStruct((copies,) + parts.shape[1:], jnp.bfloat16),
        [vmem] + [anywhere] * len(after),
        cost=(parts.size, 2 * parts.size),
    )(parts, *after)


def placed(source, shape):
    sides = source.shape[0]
    return pl.pallas_call(
        finish_kernel,
        out_shape=jax.ShapeDtypeStruct(shape, jnp.float32),
        in_specs=[vmem],
        out_specs=anywhere,
        scratch_shapes=[
            pltpu.VMEM((sides,) + shape[:2] + (shape[2] // sides,), jnp.float32),
            pltpu.SemaphoreType.DMA((sides,)),
        ],
        cost_estimate=pl.CostEstimate(
            flops=source.size, bytes_accessed=6 * source.size, transcendentals=0
        ),
        compiler_params=pltpu.CompilerParams(vmem_limit_bytes=32 * 1024 * 1024),
    )(source)


def local(features, kernel, noise_seed, noise_table, truth, area_weight):
    feature_map = features[0, 0]
    hidden, rows, cols = feature_map.shape
    chans = kernel.shape[3]
    members = lax.axis_size("member")
    place = lax.axis_index("member")
    bf16, f32 = jnp.bfloat16, jnp.float32

    x_low, x_high = neighbours(feature_map[:, 0, :], feature_map[:, rows - 1, :])
    x_rows = jnp.transpose(feature_map, (1, 0, 2))
    weights = jnp.pad(
        jnp.transpose(kernel, (0, 1, 3, 2)), ((0, 0), (0, 0), (0, padded_chans - chans), (0, 0))
    ).reshape(9 * padded_chans, hidden)
    offset = jnp.pad(
        lax.dynamic_slice(noise_table, (noise_seed[0, 0], 0), (1, chans))[0],
        (0, padded_chans - chans),
    )
    offset = jnp.broadcast_to(offset[:, None], (padded_chans, lanes))
    own_truth = jnp.pad(truth[0], ((0, padded_chans - chans), (0, 0), (0, 0)))
    own_truth = lax.dynamic_slice(
        own_truth, ((place % 2) * half_chans, place // 2, 0), (half_chans, 1, cols)
    )[:, 0, :].astype(f32)
    inner = call(
        inner_kernel,
        jax.ShapeDtypeStruct((members, half_chans, cols), f32),
        [vmem] * 3 + [anywhere],
        cost=(2 * hidden * 9 * chans * rows * cols, 4 * hidden * rows * cols),
    )(x_rows, weights, offset, own_truth)
    predicted = call(
        edge_kernel,
        jax.ShapeDtypeStruct((members, half_chans, cols), f32),
        [vmem] * 4,
        cost=(4 * hidden * 3 * chans * cols, 4 * hidden * cols),
    )(inner, x_high, x_low, weights)

    eps_value = (1.0 - alpha_level) / members
    coef = (1.0 - eps_value) / (members - 1)
    deltas = call(
        functools.partial(pair_kernel, coef),
        jax.ShapeDtypeStruct((members, half_chans, cols), bf16),
        [vmem] * 3,
        [pltpu.VMEM((members, half_chans, cols), f32)],
        cost=(members * members * 8 * half_chans * cols, 6 * members * half_chans * cols),
    )(exchange(predicted, "member"), own_truth, area_weight[None])
    delta = exchange(deltas, "member")

    d_low, d_high = neighbours(delta[:2], delta[members - 2 :])
    group = padded_rows // 8
    piece = jax.ShapeDtypeStruct((members, group, lanes), bf16)
    flops = hidden * 9 * chans * rows * cols
    sent, wide_delta = call(
        sent_kernel,
        [piece, jax.ShapeDtypeStruct((taps_chans, rows * cols), bf16)],
        [vmem] * 4,
        cost=(flops, 2 * hidden * rows * cols),
    )(delta, x_rows, x_high, x_low)
    part = call(
        kept_kernel,
        piece,
        [vmem] * 5,
        cost=(flops, 2 * hidden * rows * cols),
    )(wide_delta, x_rows, x_high, x_low, lax.all_gather(sent, "rep", axis=0))
    grad_rows = call(
        feature_grad_kernel,
        jax.ShapeDtypeStruct((rows, hidden, cols), bf16),
        [vmem] * 4,
        cost=(2 * hidden * 9 * chans * rows * cols, 4 * hidden * rows * cols),
    )(weights, wide_delta, d_high, d_low)
    feature_grad = jnp.transpose(grad_rows, (1, 0, 2))[None, None]

    bands = lax.axis_size("band")
    near = 4
    far = bands // near
    nearby = [[far_step * near + step for step in range(near)] for far_step in range(far)]
    distant = [[far_step * near + step for far_step in range(far)] for step in range(near)]
    def pairs(distance):
        return [
            [base + step, base + step + distance]
            for base in range(0, bands, 2 * distance)
            for step in range(distance)
        ]

    def paired(part, distance):
        return lax.all_gather(part[0], "band", axis=0, axis_index_groups=pairs(distance))

    part = summed(exchange(part, "member"), 1)
    part = summed(paired(part, 8), 1, after=(d_high, d_low))
    part = summed(paired(part, 4), near)
    scale = 1.0 / math.sqrt(lax.axis_size("rep") * members * bands * rows * cols)
    part = summed(exchange(part, "band", nearby), members, scale, after=(feature_grad,))
    part = exchange(part, "member")
    kernel_grad = placed(lax.all_gather(part, "rep", axis=0), (9, chans, hidden))
    kernel_grad = jnp.transpose(kernel_grad.reshape(3, 3, chans, hidden), (0, 1, 3, 2))
    return (feature_grad, kernel_grad)


def solution(mesh):
    return jax.shard_map(
        local,
        mesh=mesh,
        in_specs=(
            P("rep", "member", None, "band", None),
            P(),
            P("rep", "member"),
            P(),
            P("rep", None, "band", None),
            P("band"),
        ),
        out_specs=(P("rep", "member", None, "band", None), P()),
        check_vma=False,
    )
```
